128 devices in a mesh: brick: 32 (over x, z, core), view: 4 (over y).
Axes of the slice: x: 4, y: 4, z: 4, core: 2. Of those that a mesh axis runs over, the one named last changes fastest.
Arguments:
- estimate: float32 [1024, 128, 128], P('brick'), may hold values from 0.5 to 2
- view_data: bfloat16 [8, 2048, 128, 128], P('view', 'brick'), may hold values from 0.25 to 4
- psf_taps: float32 [8, 3, 31], P('view'), may hold values from 0.05 to 1
- routes: int32 [8, 1024, 1], P('view'), may hold values from 0 to 31; in each aligned block of 32 rows (0 to 31, 32 to 63, ..., all dimensions but the last counted through in order) at most 2 rows name the same one
Outputs:
- merged: float32 [1024, 128, 128], P('brick')
The draws below stay inside these ranges and needn't reach their ends.
Inputs may be any that keep to these rules, and one draw needn't show every extreme that they name: `routes`: in each view, among the 32 planes of one brick no owner is named more than 2 times, and some brick reaches 2.
All inputs are finite; a program needn't handle non-finite values.
Results may differ from the reference program's by a relative error of at most 0.0003.
Values may be sent and summed in bfloat16 or wider, within the bound.
No kernel may reach another device: no remote copies, remote signals or barrier semaphores. Data moves between devices by JAX's collectives and lax.ppermute only.
A program may use at most 128 MiB of HBM per device.

```python
import math
import jax
import jax.numpy as jnp
import numpy as np
from jax import lax

CX = 32
CY = 128
CZ = 128
TAPS = 31
VIEWS = 8
ITERS = 2
CAP = 2
NX = 1024
N_BRICK = 32


def block_scale(own_key, shape, cuts, smallest, top_value):
    factor_of, own = 1.0, jax.random.fold_in(own_key, 6)
    for dim, parts in cuts:
        steps = jnp.exp(jax.random.uniform(jax.random.fold_in(own, dim), (parts,), jnp.float32, smallest / len(cuts), top_value / len(cuts)))
        factor_of = factor_of * jnp.repeat(steps, shape[dim] // parts).reshape([-1 if axis == dim else 1 for axis in range(len(shape))])
    return factor_of


def deal_out(own_key, own, number, rows, count, top, reach, slope):
    ranking = jax.random.permutation(own_key, count)
    crowded, ordinary = portions_of(count, rows * top, reach, slope, True), portions_of(count, rows * top, reach, slope, False)
    places = jnp.arange(count)

    def named(tallies, offset_by):
        used = int((tallies > 0).sum())
        fixed = max(1, used // 4)
        moved = fixed + (places - fixed + offset_by * (used - fixed)) % max(1, count - fixed)
        return jnp.zeros((count,), jnp.int32).at[ranking[jnp.where(places < fixed, places, moved)]].set(jnp.asarray(tallies, jnp.int32))

    tallies = jnp.where(number % 4 == 0, named(crowded, number // 4), named(ordinary, number - number // 4 - 1))
    mixed = jax.random.permutation(jax.random.fold_in(own, 3), count)
    giver, taker = mixed[0:count // 2 * 2:2], mixed[1:count // 2 * 2:2]
    margin = jnp.minimum(tallies[giver] - 1, reach - tallies[taker]) // 2
    margin = jnp.where((giver == ranking[0]) | (taker == ranking[0]) | (tallies[taker] == 0), 0, jnp.maximum(margin, 0))
    moved = jax.random.randint(jax.random.fold_in(own, 4), (count // 2,), 0, 1 << 20) % (margin + 1)
    tallies = tallies.at[giver].add(-moved).at[taker].add(moved)
    labels = jnp.searchsorted(jnp.cumsum(tallies), jnp.arange(rows * top), side="right").astype(jnp.int32)
    table = labels.reshape(top, rows).T
    table = table[jax.random.permutation(jax.random.fold_in(own, 1), rows)]
    offset_by = jax.random.randint(jax.random.fold_in(own, 2), (rows, 1), 0, top)
    return jnp.take_along_axis(table, (jnp.arange(top)[None, :] + offset_by) % top, axis=1)


def portions_of(amount, total, most, skew, full):
    portions = [(1 << 20) // math.isqrt(grade ** skew) + 1 for grade in range(1, amount + 1)]
    largest = most if full else min(most, max(-(-total // amount), total * portions[0] // sum(portions)))
    least = 1 if total - largest >= amount - 1 else 0
    counts, surplus = [largest] + [least] * (amount - 1), total - largest - least * (amount - 1)
    while surplus > 0:
        free = [i for i in range(1, amount) if counts[i] < largest] or [i for i in range(1, amount) if counts[i] < most]
        pool, remaining = sum([portions[i] for i in free]), surplus
        for i in free:
            addition = min(most - counts[i], max(1, remaining * portions[i] // pool), surplus)
            counts[i] = counts[i] + addition
            surplus = surplus - addition
    return np.array(counts)


def setup_inputs(seed: int = 0) -> dict:
    key_list = jax.random.split(jax.random.key(seed), 5)
    estimate = jnp.clip(jnp.exp(math.log(2.0) - 1.3862944 * jax.random.uniform(key_list[0], (NX, CY, CZ), jnp.float32) ** block_scale(key_list[0], (NX, CY, CZ), ((0, 32),), -0.2, 0.2)), 0.5, 2.0)
    view_data = jnp.clip(jnp.exp(math.log(4.0) - 2.7725887 * jax.random.uniform(key_list[1], (VIEWS, N_BRICK * N_BRICK * CAP, CY, CZ), jnp.float32) ** block_scale(key_list[1], (VIEWS, N_BRICK * N_BRICK * CAP, CY, CZ), ((0, 4), (1, 32)), -0.2, 0.2)), 0.25, 4.0).astype(jnp.bfloat16)
    psf_taps = jnp.clip(jnp.exp(math.log(1.0) - 2.9957323 * jax.random.uniform(key_list[2], (VIEWS, 3, TAPS), jnp.float32) ** block_scale(key_list[2], (VIEWS, 3, TAPS), ((0, 4),), -0.2, 0.2)), 0.05, 1.0)
    routes_keys = jax.random.split(jax.random.fold_in(key_list[3], 1), VIEWS * NX // CX)
    routes_turns = jax.random.permutation(jax.random.fold_in(key_list[3], 3), VIEWS * NX // CX)
    routes = jax.vmap(lambda own, number: deal_out(jax.random.fold_in(key_list[3], 2), own, number, CX, N_BRICK, 1, CAP, 2))(routes_keys, routes_turns).reshape((VIEWS, NX, 1))
    return dict(estimate=estimate, view_data=view_data, psf_taps=psf_taps, routes=routes)


highest_mode = lax.Precision.HIGHEST


def banded(tap_row, size_in, size_out, shift_by):
    width = tap_row.shape[-1]
    row_ids = jnp.arange(size_in, dtype=jnp.int32)[:, None]
    col_ids = jnp.arange(size_out, dtype=jnp.int32)[None, :]
    offset_map = row_ids - col_ids + shift_by
    selector = (offset_map[None] == jnp.arange(width, dtype=jnp.int32)[:, None, None]).astype(jnp.float32)
    return jnp.einsum("t,tji->ji", tap_row, selector, precision=highest_mode)


def blur_volume(volume, tap_rows):
    half_width = (TAPS - 1) // 2
    along_z = banded(tap_rows[2], CZ, CZ, half_width)
    along_y = banded(tap_rows[1], CY, CY, half_width)
    along_x = banded(tap_rows[0], CX + 2 * half_width, CX, 0)
    volume = jnp.einsum("xyj,ji->xyi", volume, along_z, precision=highest_mode)
    volume = jnp.einsum("xjz,ji->xiz", volume, along_y, precision=highest_mode)
    padded = jnp.pad(volume, ((half_width, half_width), (0, 0), (0, 0)))

    def one_brick(brick_id):
        slab = lax.dynamic_slice_in_dim(padded, brick_id * CX, CX + 2 * half_width, 0)
        return jnp.einsum("pyz,pi->iyz", slab, along_x, precision=highest_mode)

    stacked = lax.map(one_brick, jnp.arange(N_BRICK, dtype=jnp.int32))
    return stacked.reshape(NX, CY, CZ)


def reference(estimate, view_data, psf_taps, routes):
    normed = psf_taps / jnp.sum(psf_taps, axis=-1, keepdims=True)
    blocks = routes[..., 0].reshape(VIEWS, N_BRICK, CX)
    position = jnp.arange(CX, dtype=jnp.int32)
    earlier = position[:, None] < position[None, :]
    same_dest = (blocks[..., :, None] == blocks[..., None, :]) & earlier
    rank_in = jnp.sum(same_dest.astype(jnp.int32), axis=-2)
    source = jnp.arange(N_BRICK, dtype=jnp.int32)[None, :, None]
    slot_index = (blocks * (N_BRICK * CAP) + source * CAP + rank_in).astype(jnp.int32).reshape(VIEWS, NX)
    planes = jnp.take_along_axis(view_data, slot_index[:, :, None, None], axis=1)
    merged = estimate
    for iteration in range(ITERS):
        total_sum = jnp.zeros((NX, CY, CZ), jnp.float32)
        for view_index in range(VIEWS):
            blurred = lax.optimization_barrier(blur_volume(merged, normed[view_index]).astype(jnp.bfloat16))
            ratios = (planes[view_index].astype(jnp.float32) / blurred.astype(jnp.float32)).astype(jnp.bfloat16)
            correction = blur_volume(ratios.astype(jnp.float32), normed[view_index][:, ::-1])
            total_sum = total_sum + correction
        merged = merged * (total_sum / VIEWS)
    return merged
```

```python
from functools import partial

import jax
import jax.numpy as jnp
from jax import lax
from jax.experimental import pallas as pl
from jax.experimental.pallas import tpu as pltpu
from jax.sharding import PartitionSpec as P

VIEWS = 8
ITERS = 2
TAPS = 31
REACH = 16
BF16 = jnp.bfloat16
F32 = jnp.float32

BOTH = ("brick", "view")


def dot(a, b):
    return jnp.dot(a, b, preferred_element_type=F32)


def twice(a, axis):
    return jnp.concatenate([a, a], axis=axis)


def split(a):
    high = a.astype(BF16)
    return high, (a - high.astype(F32)).astype(BF16)


def blur_steps(fe, ax, ay, tz, t1, views, core, finish):
    ext_y = fe.shape[0]

    def along_x(step, carry):
        y0 = pl.multiple_of(step * 8, 8)
        rows = []
        for k in range(0, 8, 2):
            pair = jnp.concatenate([fe[y0 + k], fe[y0 + k + 1]], axis=1)
            out = dot(ax[...], twice(pair, 0))
            rows += [out[:, :128], out[:, 128:]]
        t1[:, pl.ds(y0, 8), :] = jnp.swapaxes(jnp.stack(rows), 0, 1)
        return carry

    lax.fori_loop(0, ext_y // 8, along_x, 0)

    def along_yz(v, carry):
        rows = []
        for i in range(0, core, 2):
            pair = jnp.concatenate([t1[v * core + i], t1[v * core + i + 1]], axis=1).astype(BF16)
            out = dot(ay[v], twice(pair, 0)).astype(BF16)
            rows += [out[:, :128], out[:, 128:]]
        plane = jnp.concatenate(rows, axis=0)
        finish(v, dot(twice(plane, 1), tz[v]))
        return carry

    lax.fori_loop(0, views, along_yz, 0)


def back_steps(ratio_of, axt, ayt, tzt, t1, out, views, core):
    def along_zy(v, carry):
        high, low = split(dot(twice(ratio_of(v), 1), tzt[v]))
        weights = twice(ayt[v], 1)
        for i in range(0, core, 2):
            here, there = slice(i * core, (i + 1) * core), slice((i + 1) * core, (i + 2) * core)
            pair = jnp.concatenate([high[here], high[there]], axis=1)
            rest = jnp.concatenate([low[here], low[there]], axis=1)
            rows = dot(weights, jnp.concatenate([pair, pair, rest, rest], axis=0))
            t1[v * core + i] = rows[:, :128]
            t1[v * core + i + 1] = rows[:, 128:]
        return carry

    lax.fori_loop(0, views, along_zy, 0)
    ext = out.shape[1]

    def along_x(step, carry):
        y0 = pl.multiple_of(step * 8, 8)
        high, low = split(jnp.swapaxes(t1[:, pl.ds(y0, 8), :], 0, 1))
        for k in range(0, 8, 2):
            both = dot(axt[...], jnp.concatenate([high[k], high[k + 1]], axis=1))
            rest = dot(axt[:ext], jnp.concatenate([low[k], low[k + 1]], axis=1))
            rows = both[:ext] + both[ext:] + rest
            out[y0 + k] = rows[:, :128]
            out[y0 + k + 1] = rows[:, 128:]
        return carry

    lax.fori_loop(0, out.shape[0] // 8, along_x, 0)


LEVEL = 272
HALF = 32768.0


def mark_of(part):
    top = jnp.max(jnp.max(part, axis=0), axis=0, keepdims=True)
    top = jnp.broadcast_to(jnp.max(top, axis=1, keepdims=True), (1, part.shape[-1]))
    return jnp.clip(jnp.ceil(jnp.log2(top)), -200.0, 200.0) + 256.0


def encode(part, mark):
    codes = jnp.round(part * jnp.exp2(LEVEL - mark)) - HALF
    return jnp.clip(codes, -HALF, HALF - 1).astype(jnp.int32).astype(jnp.int16)


def decode(codes, mark):
    mark = mark.astype(jnp.int32).astype(F32)[:1]
    scale = jnp.where(mark > 0, jnp.exp2(mark - LEVEL), 0.0)
    return (codes.astype(jnp.int32).astype(F32) + HALF) * scale


def marked(mark, like):
    return jnp.broadcast_to(mark.astype(jnp.int32), like).astype(jnp.int16)


def in_blocks(count, body):
    def step(n, carry):
        body(pl.multiple_of(n * 8, 8))
        return carry

    lax.fori_loop(0, count // 8, step, 0)


def send_part(part, codes, first):
    mark = mark_of(part[...])
    count = part.shape[0]

    def block(y):
        codes[pl.ds(first + y, 8)] = encode(part[pl.ds(y, 8)], mark)

    in_blocks(count, block)
    row = marked(mark, codes.shape[1:])
    codes[first + count] = row
    if first:
        codes[0] = row


def blur_kernel(fe, ax, ay, tz, out, t1):
    views, core = ay.shape[0], ay.shape[1]

    def finish(v, rows):
        out[v] = rows.astype(BF16)

    blur_steps(fe, ax, ay, tz, t1, views, core, finish)


def ratio_rows(v, core, where, got, den):
    rows = [got[where[v * core + x]] for x in range(core)]
    data = jnp.concatenate(rows, axis=0).astype(F32)
    return (data / den.astype(F32)).astype(BF16)


def back_kernel(where, blurred, got, axt, ayt, tzt, out, codes, t1):
    views, core = ayt.shape[0], got.shape[1]
    back_steps(
        lambda v: ratio_rows(v, core, where, got, blurred[v]), axt, ayt, tzt, t1, out, views, core
    )
    send_part(out, codes, 0)


def full_kernel(
    where, field, total, above, below, got, ax, ay, tz, axt, ayt, tzt,
    kept, out, codes, fe, fresh, t1, ratios,
):
    views, core = ay.shape[0], ay.shape[1]
    side = above.shape[0] - 1

    def renew(codes_ref, mark_row, start, first):
        def block(y):
            add = decode(codes_ref[pl.ds(start + y, 8)], codes_ref[mark_row, :16])
            rows = pl.ds(first + y, 8)
            fresh[rows] = field[rows] * ((total[rows] + add) / views)
            fe[rows] = fresh[rows].astype(BF16)

        in_blocks(side, block)

    renew(above, side, 0, 0)
    renew(below, 0, 1, side)
    kept[...] = fresh[REACH : REACH + core, REACH : REACH + core]

    def finish(v, rows):
        ratios[v] = ratio_rows(v, core, where, got, rows.astype(BF16))

    blur_steps(fe, ax, ay, tz, t1, views, core, finish)
    back_steps(lambda v: ratios[v], axt, ayt, tzt, t1, out, views, core)
    send_part(out, codes, 0)


def gather_x_kernel(part, left, right, out, codes):
    ext_y, ext_x = part.shape[:2]
    side = left.shape[1]
    off = (ext_x - 2 * side) // 2
    last = left.shape[0] - 1

    def block(y):
        rows = pl.ds(y, 8)
        for got, at in ((left, 0), (right, side)):
            add = decode(got[rows], got[last, :16])
            out[rows, at : at + side] = part[rows, off + at : off + at + side] + add

    in_blocks(ext_y, block)
    send_part(out, codes, 1)


def last_kernel(field, total, above, below, codes, fresh):
    views, side = VIEWS, above.shape[0] - 1
    core = total.shape[0] // 2

    for got, mark_row, start, first in ((above, side, 0, 0), (below, 0, 1, side)):
        def block(y):
            add = decode(got[pl.ds(start + y, 8)], got[mark_row, :16])
            part = total[pl.ds(REACH + first + y, 8)] + add
            fresh[pl.ds(first + y, 8)] = field[pl.ds(first + y, 8)] * (part / views)

        in_blocks(side, block)
    send_part(fresh, codes, 1)


def place_kernel(order, one, two, three, four, five, out):
    core = one.shape[1]
    half = core // 2

    def put(ref, mark, start, count, group, first):
        for y in range(0, count, 8):
            rows = decode(ref[start + y : start + y + 8], mark[0, :16])
            at = pl.multiple_of(group * core + first + y, 8)
            out[:, pl.ds(at, 8), :] = jnp.swapaxes(rows, 0, 1)

    put(one, one, 1, core, order[0], 0)
    put(two, two, 1, core, order[1], 0)
    put(three, three, 1, core, order[3], 0)
    put(four, four, 1, half, order[2], 0)
    put(five, four, 0, half, order[2], half)


VMEM = pl.BlockSpec(memory_space=pltpu.VMEM)
SMEM = pl.BlockSpec(memory_space=pltpu.SMEM)


def call(kernel, out_shape, scratch, flops, *operands, scalars=0):
    size = sum(a.size * a.dtype.itemsize for a in operands)
    return pl.pallas_call(
        kernel,
        out_shape=out_shape,
        in_specs=[SMEM] * scalars + [VMEM] * (len(operands) - scalars),
        out_specs=jax.tree.map(lambda _: VMEM, out_shape),
        scratch_shapes=scratch,
        compiler_params=pltpu.CompilerParams(vmem_limit_bytes=56 << 20),
        cost_estimate=pl.CostEstimate(flops=flops, bytes_accessed=size, transcendentals=0),
    )(*operands)


def halves(a, axis):
    high = lax.reduce_precision(a, 8, 7)
    return jnp.concatenate([high, a - high], axis=axis).astype(BF16)


def banded(taps, rows, cols, shift):
    offset = jnp.arange(rows)[:, None] - jnp.arange(cols)[None, :] + shift
    select = (offset[None] == jnp.arange(TAPS)[:, None, None]).astype(F32)
    return jnp.einsum("vt,trc->vrc", taps, select, precision=lax.Precision.HIGHEST)


def shifted(a, dx, dy):
    bricks, views = lax.axis_size("brick"), lax.axis_size("view")
    pairs = []
    for b in range(bricks):
        for q in range(views):
            if 0 <= b + dx < bricks and 0 <= q + dy < views:
                pairs.append((b * views + q, (b + dx) * views + q + dy))
    return lax.ppermute(a, BOTH, pairs)


def turn(count, by):
    return [(i, (i + by) % count) for i in range(count)]


def per_device(estimate, view_data, psf_taps, routes):
    bricks, groups = lax.axis_size("brick"), lax.axis_size("view")
    brick, group = lax.axis_index("brick"), lax.axis_index("view")
    planes, size_y, size_z = estimate.shape
    views_dev, slots = view_data.shape[:2]
    capacity = slots // bricks
    core = size_y // groups
    ext = core + 2 * REACH
    views = views_dev * groups

    normed = psf_taps / jnp.sum(psf_taps, axis=-1, keepdims=True)
    blocks = routes[..., 0].reshape(views_dev, bricks, planes)
    own = lax.dynamic_index_in_dim(blocks, brick, 1, keepdims=False)
    position = jnp.arange(planes)
    earlier = position[:, None] < position[None, :]
    rank = jnp.sum(((own[:, :, None] == own[:, None, :]) & earlier).astype(jnp.int32), axis=1)
    view_id = jnp.arange(views_dev)[:, None]
    where = ((own * groups + group) * views_dev + view_id) * capacity + rank
    packed = jnp.concatenate(
        [normed.reshape(views_dev, 3 * TAPS), where.astype(F32)], axis=1
    )
    packed = jnp.pad(packed, ((0, 0), (0, 128 - packed.shape[1])))
    near = [packed] + [lax.ppermute(packed, "view", turn(groups, k)) for k in range(1, groups)]
    near = jnp.concatenate([near[0]] + near[:0:-1], axis=0)
    packed = lax.dynamic_slice_in_dim(
        twice(near, 0), (groups - group) % groups * views_dev, views, 0
    )

    def window(rows):
        tall = jnp.pad(rows, ((0, 0), (REACH, REACH), (0, 0)))
        return lax.dynamic_slice_in_dim(tall, group * core, ext, 1).transpose(1, 0, 2)

    before = shifted(window(estimate[planes - REACH :].astype(BF16)), 1, 0)
    after = shifted(window(estimate[:REACH].astype(BF16)), -1, 0)

    sending = view_data.reshape(views_dev, bricks, capacity, groups, core, size_z)
    sending = sending.transpose(1, 3, 0, 2, 4, 5).reshape(
        bricks * groups, views_dev * capacity, core, size_z
    )
    sending, before, after, packed = lax.optimization_barrier((sending, before, after, packed))
    got = lax.all_to_all(sending, BOTH, 0, 0, tiled=True)
    got = got.reshape(bricks * groups * views_dev * capacity, core, size_z)

    taps = packed[:, : 3 * TAPS].reshape(views, 3, TAPS)
    where = packed[:, 3 * TAPS : 3 * TAPS + planes].astype(jnp.int32).reshape(views * planes)

    mat_x = banded(taps[:, 0], ext, planes, -1)
    mat_y = banded(taps[:, 1], ext, core, -1)
    mat_z = banded(taps[:, 2], size_z, size_z, TAPS // 2)
    ax = halves(mat_x.transpose(0, 2, 1).reshape(views * planes, ext), 1)
    ay = halves(mat_y.transpose(0, 2, 1), 2)
    tz = halves(mat_z, 1)
    axt = halves(mat_x.transpose(1, 0, 2).reshape(ext, views * planes), 0)
    ayt = halves(mat_y, 2)
    tzt = halves(mat_z.transpose(0, 2, 1), 1)

    field = window(estimate)
    field = jnp.concatenate([before.astype(F32), field, after.astype(F32)], axis=1)

    scratch = pltpu.VMEM((views * planes, ext, size_z), F32)

    def shape(*dims):
        return jax.ShapeDtypeStruct(dims + (size_z,), F32)

    def codes(*dims):
        return jax.ShapeDtypeStruct(dims + (size_z,), jnp.int16)

    flops = 4 * 10**9
    rows_shape = (views, planes * core, size_z)
    blurred = call(
        blur_kernel,
        jax.ShapeDtypeStruct(rows_shape, BF16),
        [scratch],
        flops,
        field.astype(BF16),
        ax,
        ay,
        tz,
    )
    part, sent = call(
        back_kernel,
        (shape(ext, ext), codes(ext + 1, ext)),
        [scratch],
        flops,
        where,
        blurred,
        got,
        axt,
        ayt,
        tzt,
        scalars=1,
    )
    side = 2 * REACH
    left = shifted(sent[:, planes:], 1, 0)
    right = shifted(sent[:, :side], -1, 0)
    total, sent = call(
        gather_x_kernel,
        (shape(ext, ext), codes(ext + 2, ext)),
        [],
        0,
        part,
        left,
        right,
    )
    above = shifted(sent[core + 1 :], 0, 1)
    below = shifted(sent[: side + 1], 0, -1)
    field, part, sent = call(
        full_kernel,
        (shape(core, planes), shape(ext, ext), codes(ext + 1, ext)),
        [
            pltpu.VMEM((ext, ext, size_z), BF16),
            pltpu.VMEM((ext, ext, size_z), F32),
            scratch,
            pltpu.VMEM(rows_shape, BF16),
        ],
        2 * flops,
        where,
        field,
        total,
        above,
        below,
        got,
        ax,
        ay,
        tz,
        axt,
        ayt,
        tzt,
        scalars=1,
    )
    side = REACH
    left = shifted(sent[:, planes + side :], 1, 0)
    right = shifted(sent[:, :side], -1, 0)
    total, sent = call(
        gather_x_kernel,
        (shape(ext, planes), codes(ext + 2, planes)),
        [],
        0,
        part,
        left,
        right,
    )
    above = shifted(sent[core + side + 1 :], 0, 1)
    below = shifted(sent[: side + 1], 0, -1)
    sent = call(
        last_kernel,
        codes(core + 2, planes),
        [pltpu.VMEM((core, planes, size_z), F32)],
        0,
        field,
        total,
        above,
        below,
    )
    sent = sent[: core + 1]
    half = core // 2 + 1
    up, down = turn(groups, 1), turn(groups, -1)
    before, after = lax.ppermute(sent, "view", up), lax.ppermute(sent, "view", down)
    first, second = lax.ppermute(before[:half], "view", up), lax.ppermute(after[half:], "view", down)
    order = (group - jnp.arange(groups)) % groups
    return call(
        place_kernel,
        shape(planes, size_y),
        [],
        0,
        order,
        sent,
        before,
        after,
        first,
        second,
        scalars=1,
    )


def solution(mesh):
    return jax.shard_map(
        per_device,
        mesh=mesh,
        in_specs=(
            P("brick", None, None),
            P("view", "brick", None, None),
            P("view", None, None),
            P("view", None, None),
        ),
        out_specs=P("brick", None, None),
        check_vma=False,
    )
```

```python
from functools import partial

import jax
import jax.numpy as jnp
from jax import lax
from jax.experimental import pallas as pl
from jax.experimental.pallas import tpu as pltpu
from jax.sharding import PartitionSpec as P

VIEWS = 8
ITERS = 2
TAPS = 31
REACH = 16
BF16 = jnp.bfloat16
F32 = jnp.float32

BOTH = ("brick", "view")


def dot(a, b):
    return jnp.dot(a, b, preferred_element_type=F32)


def twice(a, axis):
    return jnp.concatenate([a, a], axis=axis)


def split(a):
    high = a.astype(BF16)
    return high, (a - high.astype(F32)).astype(BF16)


def blur_steps(fe, ax, ay, tz, t1, views, core, finish):
    ext_y = fe.shape[0]

    def along_x(step, carry):
        y0 = pl.multiple_of(step * 8, 8)
        rows = []
        for k in range(0, 8, 2):
            pair = jnp.concatenate([fe[y0 + k], fe[y0 + k + 1]], axis=1)
            out = dot(ax[...], twice(pair, 0))
            rows += [out[:, :128], out[:, 128:]]
        t1[:, pl.ds(y0, 8), :] = jnp.swapaxes(jnp.stack(rows), 0, 1)
        return carry

    lax.fori_loop(0, ext_y // 8, along_x, 0, unroll=True)

    def along_yz(v, carry):
        rows = []
        for i in range(0, core, 2):
            pair = jnp.concatenate([t1[v * core + i], t1[v * core + i + 1]], axis=1).astype(BF16)
            out = dot(ay[v], twice(pair, 0)).astype(BF16)
            rows += [out[:, :128], out[:, 128:]]
        plane = jnp.concatenate(rows, axis=0)
        finish(v, dot(twice(plane, 1), tz[v]))
        return carry

    lax.fori_loop(0, views, along_yz, 0, unroll=True)


def back_steps(ratio_of, axt, ayt, tzt, t1, out, views, core):
    def along_zy(v, carry):
        high, low = split(dot(twice(ratio_of(v), 1), tzt[v]))
        weights = twice(ayt[v], 1)
        for i in range(0, core, 2):
            here, there = slice(i * core, (i + 1) * core), slice((i + 1) * core, (i + 2) * core)
            pair = jnp.concatenate([high[here], high[there]], axis=1)
            rest = jnp.concatenate([low[here], low[there]], axis=1)
            rows = dot(weights, jnp.concatenate([pair, pair, rest, rest], axis=0))
            t1[v * core + i] = rows[:, :128]
            t1[v * core + i + 1] = rows[:, 128:]
        return carry

    lax.fori_loop(0, views, along_zy, 0, unroll=True)
    ext = out.shape[1]

    def along_x(step, carry):
        y0 = pl.multiple_of(step * 8, 8)
        high, low = split(jnp.swapaxes(t1[:, pl.ds(y0, 8), :], 0, 1))
        for k in range(0, 8, 2):
            both = dot(axt[...], jnp.concatenate([high[k], high[k + 1]], axis=1))
            rest = dot(axt[:ext], jnp.concatenate([low[k], low[k + 1]], axis=1))
            rows = both[:ext] + both[ext:] + rest
            out[y0 + k] = rows[:, :128]
            out[y0 + k + 1] = rows[:, 128:]
        return carry

    lax.fori_loop(0, out.shape[0] // 8, along_x, 0, unroll=True)


SHIFT = 256.0
LEVELS = 65534.0
HALF = 32767


def mark_of(part):
    top = jnp.max(jnp.max(part, axis=0), axis=0, keepdims=True)
    top = jnp.broadcast_to(jnp.max(top, axis=1, keepdims=True), (1, part.shape[-1]))
    return jnp.clip(jnp.ceil(jnp.log2(top)), -100.0, 120.0) + SHIFT


def encode(part, scale):
    return ((part * scale + 0.5).astype(jnp.int32) - HALF).astype(jnp.int16)


def decode(codes, scale):
    return (codes.astype(jnp.int32) + HALF).astype(F32) * scale


def scale_of(message):
    mark = message[message.shape[0] - 1, :16].astype(jnp.int32).astype(F32)[:1]
    return jnp.where(mark > 0, jnp.exp2(mark - SHIFT) / LEVELS, 0.0)


def in_blocks(count, body):
    def step(n, carry):
        body(pl.multiple_of(n * 8, 8))
        return carry

    lax.fori_loop(0, count // 8, step, 0)


def send_part(part, *messages):
    mark = mark_of(part[...])
    scale = jnp.exp2(SHIFT - mark) * LEVELS
    for out, y0, x0 in messages:
        count, width = out.shape[0] - 1, out.shape[1]

        def block(y):
            out[pl.ds(y, 8)] = encode(part[pl.ds(y0 + y, 8), x0 : x0 + width], scale)

        in_blocks(count, block)
        out[count] = jnp.broadcast_to(mark.astype(jnp.int32), out.shape[1:]).astype(jnp.int16)


def prepare_kernel(group, estimate, core, up, down):
    planes, size_y = estimate.shape[:2]
    count = core.shape[0]
    first = group[0] * (count - 2 * REACH) - REACH
    for y in range(0, count, 8):
        at = first + y
        inside = jnp.logical_and(at >= 0, at < size_y)
        rows = estimate[:, pl.ds(pl.multiple_of(jnp.clip(at, 0, size_y - 8), 8), 8), :]
        rows = jnp.where(inside, jnp.swapaxes(rows, 0, 1), 0.0)
        core[y : y + 8] = rows
        up[y : y + 8] = rows[:, planes - REACH :].astype(BF16)
        down[y : y + 8] = rows[:, :REACH].astype(BF16)


def deal_kernel(data, out, sems):
    views, groups, core = data.shape[0], out.shape[1], out.shape[4]
    copies = []
    for v in range(views):
        for q in range(groups):
            copies.append(
                pltpu.make_async_copy(
                    data.at[v, :, :, q * core : (q + 1) * core, :],
                    out.at[:, q, v],
                    sems.at[v * groups + q],
                )
            )
    for copy in copies:
        copy.start()
    for copy in copies:
        copy.wait()


def blur_kernel(before, middle, after, ax, ay, tz, out, fe, t1):
    views, core = ay.shape[0], ay.shape[1]

    def block(y):
        rows = pl.ds(y, 8)
        fe[rows, :REACH] = before[rows]
        fe[rows, REACH : REACH + core] = middle[rows].astype(BF16)
        fe[rows, REACH + core :] = after[rows]

    in_blocks(fe.shape[0], block)

    def finish(v, rows):
        out[v] = rows.astype(BF16)

    blur_steps(fe, ax, ay, tz, t1, views, core, finish)


def ratio_rows(v, core, where, got, den):
    rows = [got[where[v * core + x]] for x in range(core)]
    data = jnp.concatenate(rows, axis=0).astype(F32)
    return (data / den.astype(F32)).astype(BF16)


def back_kernel(where, blurred, got, axt, ayt, tzt, out, right, left, t1):
    views, core = ayt.shape[0], got.shape[1]
    back_steps(
        lambda v: ratio_rows(v, core, where, got, blurred[v]), axt, ayt, tzt, t1, out, views, core
    )
    send_part(out, (right, 0, out.shape[1] - right.shape[1]), (left, 0, 0))


def full_kernel(
    where, before, middle, after, total, above, below, got, ax, ay, tz, axt, ayt, tzt,
    kept, out, right, left, fe, t1, ratios,
):
    views, core = ay.shape[0], ay.shape[1]
    side = above.shape[0] - 1

    for codes, first in ((above, 0), (below, side)):
        scale = scale_of(codes)

        def block(y):
            rows = pl.ds(first + y, 8)
            step = (total[rows] + decode(codes[pl.ds(y, 8)], scale)) / views
            field = jnp.concatenate(
                [before[rows].astype(F32), middle[rows], after[rows].astype(F32)], axis=1
            )
            fresh = field * step
            fe[rows] = fresh.astype(BF16)
            kept[rows] = fresh[:, REACH : REACH + core]

        in_blocks(side, block)

    def finish(v, rows):
        ratios[v] = ratio_rows(v, core, where, got, rows.astype(BF16))

    blur_steps(fe, ax, ay, tz, t1, views, core, finish)
    back_steps(lambda v: ratios[v], axt, ayt, tzt, t1, out, views, core)
    send_part(out, (right, 0, out.shape[1] - right.shape[1]), (left, 0, 0))


def gather_x_kernel(part, left, right, out, up, down):
    ext_y, ext_x = part.shape[:2]
    side = left.shape[1]
    off = (ext_x - 2 * side) // 2
    scale_l, scale_r = scale_of(left), scale_of(right)

    def block(y):
        rows = pl.ds(y, 8)
        for got, scale, at in ((left, scale_l, 0), (right, scale_r, side)):
            add = decode(got[rows], scale)
            out[rows, at : at + side] = part[rows, off + at : off + at + side] + add

    in_blocks(ext_y, block)
    send_part(out, (up, ext_y - up.shape[0] + 1, 0), (down, 0, 0))


def last_kernel(field, total, above, below, codes, fresh):
    side = above.shape[0] - 1
    for got, first in ((above, 0), (below, side)):
        scale = scale_of(got)

        def block(y):
            rows = pl.ds(REACH + first + y, 8)
            step = (total[rows] + decode(got[pl.ds(y, 8)], scale)) / VIEWS
            fresh[pl.ds(first + y, 8)] = field[rows] * step

        in_blocks(side, block)
    send_part(fresh, (codes, 0, 0))


def place_kernel(order, one, two, three, four, five, out):
    core = one.shape[1]
    half = core // 2

    def put(ref, scale, count, group, first):
        for y in range(0, count, 8):
            rows = decode(ref[y : y + 8], scale)
            at = pl.multiple_of(group * core + first + y, 8)
            out[:, pl.ds(at, 8), :] = jnp.swapaxes(rows, 0, 1)

    put(one, scale_of(one), core, order[0], 0)
    put(two, scale_of(two), core, order[1], 0)
    put(three, scale_of(three), core, order[3], 0)
    put(four, scale_of(five), half, order[2], 0)
    put(five, scale_of(five), half, order[2], half)


VMEM = pl.BlockSpec(memory_space=pltpu.VMEM)
SMEM = pl.BlockSpec(memory_space=pltpu.SMEM)


def call(kernel, out_shape, scratch, flops, *operands, scalars=0, space=VMEM):
    size = sum(a.size * a.dtype.itemsize for a in operands)
    return pl.pallas_call(
        kernel,
        out_shape=out_shape,
        in_specs=[SMEM] * scalars + [space] * (len(operands) - scalars),
        out_specs=jax.tree.map(lambda _: space, out_shape),
        scratch_shapes=scratch,
        compiler_params=pltpu.CompilerParams(vmem_limit_bytes=36 << 20),
        cost_estimate=pl.CostEstimate(flops=flops, bytes_accessed=size, transcendentals=0),
    )(*operands)


def halves(a, axis):
    high = lax.reduce_precision(a, 8, 7)
    return jnp.concatenate([high, a - high], axis=axis).astype(BF16)


def banded(taps, rows, cols, shift):
    offset = jnp.arange(rows)[:, None] - jnp.arange(cols)[None, :] + shift
    select = (offset[None] == jnp.arange(TAPS)[:, None, None]).astype(F32)
    return jnp.einsum("vt,trc->vrc", taps, select, precision=lax.Precision.HIGHEST)


def shifted(a, dx, dy):
    bricks, views = lax.axis_size("brick"), lax.axis_size("view")
    pairs = []
    for b in range(bricks):
        for q in range(views):
            if 0 <= b + dx < bricks and 0 <= q + dy < views:
                pairs.append((b * views + q, (b + dx) * views + q + dy))
    return lax.ppermute(a, BOTH, pairs)


def turn(count, by):
    return [(i, (i + by) % count) for i in range(count)]


def per_device(estimate, view_data, psf_taps, routes):
    bricks, groups = lax.axis_size("brick"), lax.axis_size("view")
    brick, group = lax.axis_index("brick"), lax.axis_index("view")
    planes, size_y, size_z = estimate.shape
    views_dev, slots = view_data.shape[:2]
    capacity = slots // bricks
    core = size_y // groups
    ext = core + 2 * REACH
    views = views_dev * groups

    normed = psf_taps / jnp.sum(psf_taps, axis=-1, keepdims=True)
    blocks = routes[..., 0].reshape(views_dev, bricks, planes)
    own = lax.dynamic_index_in_dim(blocks, brick, 1, keepdims=False)
    position = jnp.arange(planes)
    earlier = position[:, None] < position[None, :]
    rank = jnp.sum(((own[:, :, None] == own[:, None, :]) & earlier).astype(jnp.int32), axis=1)
    view_id = jnp.arange(views_dev)[:, None]
    where = ((own * groups + group) * views_dev + view_id) * capacity + rank
    packed = jnp.concatenate(
        [normed.reshape(views_dev, 3 * TAPS), where.astype(F32)], axis=1
    )
    packed = jnp.pad(packed, ((0, 0), (0, 128 - packed.shape[1])))
    near = [packed] + [lax.ppermute(packed, "view", turn(groups, k)) for k in range(1, groups)]
    near = jnp.concatenate([near[0]] + near[:0:-1], axis=0)
    packed = lax.dynamic_slice_in_dim(
        twice(near, 0), (groups - group) % groups * views_dev, views, 0
    )

    def shape(*dims, kind=F32):
        return jax.ShapeDtypeStruct(dims + (size_z,), kind)

    middle, up, down = call(
        prepare_kernel,
        (shape(ext, planes), shape(ext, REACH, kind=BF16), shape(ext, REACH, kind=BF16)),
        [],
        0,
        group.reshape(1),
        estimate,
        scalars=1,
    )
    before, after = shifted(up, 1, 0), shifted(down, -1, 0)

    sending = call(
        deal_kernel,
        shape(bricks, groups, views_dev, capacity, core, kind=BF16),
        [pltpu.SemaphoreType.DMA((views_dev * groups,))],
        0,
        view_data.reshape(views_dev, bricks, capacity, size_y, size_z),
        space=pl.BlockSpec(memory_space=pl.ANY),
    )
    sending = sending.reshape(bricks * groups, views_dev * capacity, core, size_z)
    sending, before, after, packed = lax.optimization_barrier((sending, before, after, packed))
    got = lax.all_to_all(sending, BOTH, 0, 0, tiled=True)
    got = got.reshape(bricks * groups * views_dev * capacity, core, size_z)

    taps = packed[:, : 3 * TAPS].reshape(views, 3, TAPS)
    where = packed[:, 3 * TAPS : 3 * TAPS + planes].astype(jnp.int32).reshape(views * planes)

    mat_x = banded(taps[:, 0], ext, planes, -1)
    mat_y = banded(taps[:, 1], ext, core, -1)
    mat_z = banded(taps[:, 2], size_z, size_z, TAPS // 2)
    ax = halves(mat_x.transpose(0, 2, 1).reshape(views * planes, ext), 1)
    ay = halves(mat_y.transpose(0, 2, 1), 2)
    tz = halves(mat_z, 1)
    axt = halves(mat_x.transpose(1, 0, 2).reshape(ext, views * planes), 0)
    ayt = halves(mat_y, 2)
    tzt = halves(mat_z.transpose(0, 2, 1), 1)

    scratch = pltpu.VMEM((views * planes, ext, size_z), F32)
    wide = pltpu.VMEM((ext, ext, size_z), BF16)
    codes = partial(shape, kind=jnp.int16)
    flops = 4 * 10**9
    rows_shape = (views, planes * core, size_z)
    forward, back = (ax, ay, tz), (axt, ayt, tzt)
    field = (before, middle, after)

    blurred = call(
        blur_kernel, jax.ShapeDtypeStruct(rows_shape, BF16), [wide, scratch], flops, *field, *forward
    )
    side = 2 * REACH
    part, right, left = call(
        back_kernel,
        (shape(ext, ext), codes(ext + 1, side), codes(ext + 1, side)),
        [scratch],
        flops,
        where,
        blurred,
        got,
        *back,
        scalars=1,
    )
    total, up, down = call(
        gather_x_kernel,
        (shape(ext, ext), codes(side + 1, ext), codes(side + 1, ext)),
        [],
        0,
        part,
        shifted(right, 1, 0),
        shifted(left, -1, 0),
    )
    side = REACH
    kept, part, right, left = call(
        full_kernel,
        (shape(ext, planes), shape(ext, ext), codes(ext + 1, side), codes(ext + 1, side)),
        [wide, scratch, pltpu.VMEM(rows_shape, BF16)],
        2 * flops,
        where,
        *field,
        total,
        shifted(up, 0, 1),
        shifted(down, 0, -1),
        got,
        *forward,
        *back,
        scalars=1,
    )
    total, up, down = call(
        gather_x_kernel,
        (shape(ext, planes), codes(side + 1, planes), codes(side + 1, planes)),
        [],
        0,
        part,
        shifted(right, 1, 0),
        shifted(left, -1, 0),
    )
    sent = call(
        last_kernel,
        codes(core + 1, planes),
        [pltpu.VMEM((core, planes, size_z), F32)],
        0,
        kept,
        total,
        shifted(up, 0, 1),
        shifted(down, 0, -1),
    )
    half = core // 2
    up, down = turn(groups, 1), turn(groups, -1)
    before, after = lax.ppermute(sent, "view", up), lax.ppermute(sent, "view", down)
    first, second = lax.ppermute(before[:half], "view", up), lax.ppermute(after[half:], "view", down)
    order = (group - jnp.arange(groups)) % groups
    return call(
        place_kernel,
        shape(planes, size_y),
        [],
        0,
        order,
        sent,
        before,
        after,
        first,
        second,
        scalars=1,
    )


def solution(mesh):
    return jax.shard_map(
        per_device,
        mesh=mesh,
        in_specs=(
            P("brick", None, None),
            P("view", "brick", None, None),
            P("view", None, None),
            P("view", None, None),
        ),
        out_specs=P("brick", None, None),
        check_vma=False,
    )
```

```python
from functools import partial

import jax
import jax.numpy as jnp
from jax import lax
from jax.experimental import pallas as pl
from jax.experimental.pallas import tpu as pltpu
from jax.sharding import PartitionSpec as P

VIEWS = 8
ITERS = 2
TAPS = 31
REACH = 16
BF16 = jnp.bfloat16
F32 = jnp.float32

BOTH = ("brick", "view")


def dot(a, b):
    return jnp.dot(a, b, preferred_element_type=F32)


def twice(a, axis):
    return jnp.concatenate([a, a], axis=axis)


def split(a):
    high = a.astype(BF16)
    return high, (a - high.astype(F32)).astype(BF16)


def blur_steps(fe, ax, ay, tz, t1, views, core, finish):
    ext_y = fe.shape[0]

    def along_x(step, carry):
        y0 = pl.multiple_of(step * 8, 8)
        rows = []
        for k in range(0, 8, 2):
            pair = jnp.concatenate([fe[y0 + k], fe[y0 + k + 1]], axis=1)
            out = dot(ax[...], twice(pair, 0))
            rows += [out[:, :128], out[:, 128:]]
        t1[:, pl.ds(y0, 8), :] = jnp.swapaxes(jnp.stack(rows), 0, 1)
        return carry

    lax.fori_loop(0, ext_y // 8, along_x, 0, unroll=True)

    def along_yz(v, carry):
        rows = []
        for i in range(0, core, 2):
            pair = jnp.concatenate([t1[v * core + i], t1[v * core + i + 1]], axis=1).astype(BF16)
            out = dot(ay[v], twice(pair, 0)).astype(BF16)
            rows += [out[:, :128], out[:, 128:]]
        plane = jnp.concatenate(rows, axis=0)
        finish(v, dot(twice(plane, 1), tz[v]))
        return carry

    lax.fori_loop(0, views, along_yz, 0, unroll=True)


def back_steps(ratio_of, axt, ayt, tzt, t1, out, views, core):
    def along_zy(v, carry):
        high, low = split(dot(twice(ratio_of(v), 1), tzt[v]))
        weights = twice(ayt[v], 1)
        for i in range(0, core, 2):
            here, there = slice(i * core, (i + 1) * core), slice((i + 1) * core, (i + 2) * core)
            pair = jnp.concatenate([high[here], high[there]], axis=1)
            rest = jnp.concatenate([low[here], low[there]], axis=1)
            rows = dot(weights, jnp.concatenate([pair, pair, rest, rest], axis=0))
            t1[v * core + i] = rows[:, :128]
            t1[v * core + i + 1] = rows[:, 128:]
        return carry

    lax.fori_loop(0, views, along_zy, 0, unroll=True)
    ext = out.shape[1]

    def along_x(step, carry):
        y0 = pl.multiple_of(step * 8, 8)
        high, low = split(jnp.swapaxes(t1[:, pl.ds(y0, 8), :], 0, 1))
        for k in range(0, 8, 2):
            both = dot(axt[...], jnp.concatenate([high[k], high[k + 1]], axis=1))
            rest = dot(axt[:ext], jnp.concatenate([low[k], low[k + 1]], axis=1))
            rows = both[:ext] + both[ext:] + rest
            out[y0 + k] = rows[:, :128]
            out[y0 + k + 1] = rows[:, 128:]
        return carry

    lax.fori_loop(0, out.shape[0] // 8, along_x, 0, unroll=True)


SHIFT = 256.0
LEVELS = 65534.0
HALF = 32767


def mark_of(part):
    top = jnp.max(jnp.max(part, axis=0), axis=0, keepdims=True)
    top = jnp.broadcast_to(jnp.max(top, axis=1, keepdims=True), (1, part.shape[-1]))
    return jnp.clip(jnp.ceil(jnp.log2(top)), -100.0, 120.0) + SHIFT


def encode(part, scale):
    return ((part * scale + 0.5).astype(jnp.int32) - HALF).astype(jnp.int16)


def decode(codes, scale):
    return (codes.astype(jnp.int32) + HALF).astype(F32) * scale


def scale_of(message):
    mark = message[message.shape[0] - 1, :16].astype(jnp.int32).astype(F32)[:1]
    return jnp.where(mark > 0, jnp.exp2(mark - SHIFT) / LEVELS, 0.0)


def in_blocks(count, body):
    def step(n, carry):
        body(pl.multiple_of(n * 8, 8))
        return carry

    lax.fori_loop(0, count // 8, step, 0)


def send_part(part, *messages):
    mark = mark_of(part[...])
    scale = jnp.exp2(SHIFT - mark) * LEVELS
    for out, y0, x0 in messages:
        count, width = out.shape[0] - 1, out.shape[1]

        def block(y):
            out[pl.ds(y, 8)] = encode(part[pl.ds(y0 + y, 8), x0 : x0 + width], scale)

        in_blocks(count, block)
        out[count] = jnp.broadcast_to(mark.astype(jnp.int32), out.shape[1:]).astype(jnp.int16)


def sides(odd, last):
    return (1 - odd) * last, odd * last


def for_parity(odd, body):
    for value in (0, 1):
        pl.when(odd == value)(partial(body, value))


def prepare_kernel(place, estimate, middle, near, far):
    planes, size_y = estimate.shape[:2]
    count = middle.shape[0]
    first = place[0] * (count - 2 * REACH) - REACH
    for y in range(0, count, 8):
        at = first + y
        inside = jnp.logical_and(at >= 0, at < size_y)
        rows = estimate[:, pl.ds(pl.multiple_of(jnp.clip(at, 0, size_y - 8), 8), 8), :]
        middle[y : y + 8] = jnp.where(inside, jnp.swapaxes(rows, 0, 1), 0.0)

    def send(odd):
        x_near, x_far = sides(odd, planes - REACH)
        near[...] = middle[:, x_near : x_near + REACH].astype(BF16)
        far[...] = middle[:, x_far : x_far + REACH].astype(BF16)

    for_parity(place[1], send)


def deal_kernel(data, out, stage, sems):
    views, groups, core = data.shape[0], out.shape[1], out.shape[4]
    parts = [(v, q) for v in range(views) for q in range(groups)]
    loads, stores = [], []
    for n, (v, q) in enumerate(parts):
        rows = data.at[v, :, :, q * core : (q + 1) * core, :]
        loads.append(pltpu.make_async_copy(rows, stage.at[n], sems.at[0, n]))
        stores.append(pltpu.make_async_copy(stage.at[n], out.at[:, q, v], sems.at[1, n]))
    for load in loads:
        load.start()
    for load, store in zip(loads, stores):
        load.wait()
        store.start()
    for store in stores:
        store.wait()


def blur_kernel(place, near, middle, far, ax, ay, tz, out, fe, t1):
    views, core = ay.shape[0], ay.shape[1]

    def join(odd):
        x_near, x_far = sides(odd, REACH + core)
        fe[:, x_near : x_near + REACH] = near[...]
        fe[:, REACH : REACH + core] = middle[...].astype(BF16)
        fe[:, x_far : x_far + REACH] = far[...]

    for_parity(place[1], join)

    def finish(v, rows):
        out[v] = rows.astype(BF16)

    blur_steps(fe, ax, ay, tz, t1, views, core, finish)


def ratio_rows(v, core, where, got, den):
    rows = [got[where[v * core + x]] for x in range(core)]
    data = jnp.concatenate(rows, axis=0).astype(F32)
    return (data / den.astype(F32)).astype(BF16)


def back_kernel(place, where, blurred, got, axt, ayt, tzt, out, nn, fn, nf, ff, t1):
    views, core = ayt.shape[0], got.shape[1]
    back_steps(
        lambda v: ratio_rows(v, core, where, got, blurred[v]), axt, ayt, tzt, t1, out, views, core
    )
    y_near, y_far = sides(place[2], out.shape[0] // 2)

    def send(odd):
        x_near, x_far = sides(odd, out.shape[1] - nn.shape[1])
        send_part(
            out, (nn, y_near, x_near), (fn, y_near, x_far), (nf, y_far, x_near), (ff, y_far, x_far)
        )

    for_parity(place[1], send)


def full_kernel(
    place, where, near, middle, far, total_near, total_far, got_near, got_far,
    got, ax, ay, tz, axt, ayt, tzt, kept, out, send_near, send_far, fe, t1, ratios,
):
    views, core = ay.shape[0], ay.shape[1]
    y_near, y_far = sides(place[2], out.shape[0] // 2)

    def renew(odd):
        x_near, x_far = sides(odd, REACH + core)
        fields = (near, x_near, REACH), (far, x_far, REACH), (middle, REACH, core)
        for codes, total, first in ((got_near, total_near, y_near), (got_far, total_far, y_far)):
            scale = scale_of(codes)

            def block(y):
                rows, here = pl.ds(first + y, 8), pl.ds(y, 8)
                for field, x, width in fields:
                    cells = slice(x, x + width)
                    step = (total[here, cells] + decode(codes[here, cells], scale)) / views
                    fresh = field[rows].astype(F32) * step
                    fe[rows, cells] = fresh.astype(BF16)
                    if field is middle:
                        kept[rows] = fresh

            in_blocks(total.shape[0], block)

    for_parity(place[1], renew)

    def finish(v, rows):
        ratios[v] = ratio_rows(v, core, where, got, rows.astype(BF16))

    blur_steps(fe, ax, ay, tz, t1, views, core, finish)
    back_steps(lambda v: ratios[v], axt, ayt, tzt, t1, out, views, core)

    def send(odd):
        x_near, x_far = sides(odd, out.shape[1] - REACH)
        send_part(out, (send_near, 0, x_near), (send_far, 0, x_far))

    for_parity(place[1], send)


def gather_rows(place, first, part, near, far, out):
    side = near.shape[1]
    off = (part.shape[1] - 2 * side) // 2
    scale_n, scale_f = scale_of(near), scale_of(far)

    def add_both(odd):
        x_near, x_far = sides(odd, side)

        def block(y):
            rows = pl.ds(y, 8)
            for got, scale, x in ((near, scale_n, x_near), (far, scale_f, x_far)):
                here = part[pl.ds(first + y, 8), off + x : off + x + side]
                out[rows, x : x + side] = here + decode(got[rows], scale)

        in_blocks(out.shape[0], block)

    for_parity(place[1], add_both)


def gather_half_kernel(which, place, part, near, far, out, message):
    gather_rows(place, sides(place[2], part.shape[0] // 2)[which], part, near, far, out)
    send_part(out, (message, 0, 0))


def gather_all_kernel(place, part, near, far, out, send_near, send_far):
    gather_rows(place, 0, part, near, far, out)
    y_near, y_far = sides(place[2], part.shape[0] - REACH)
    send_part(out, (send_near, y_near, 0), (send_far, y_far, 0))


def last_kernel(place, field, total, near, far, codes_lo, codes_hi, fresh):
    y_near, y_far = sides(place[2], REACH)
    for got, first in ((near, y_near), (far, y_far)):
        scale = scale_of(got)

        def block(y):
            rows = pl.ds(REACH + first + y, 8)
            step = (total[rows] + decode(got[pl.ds(y, 8)], scale)) / VIEWS
            fresh[pl.ds(first + y, 8)] = field[rows] * step

        in_blocks(REACH, block)
    send_part(fresh, (codes_lo, 0, 0), (codes_hi, fresh.shape[0] // 2, 0))


def place_rows(message, write):
    scale = scale_of(message)
    for y in range(0, message.shape[0] - 1, 8):
        write(y, jnp.swapaxes(decode(message[y : y + 8], scale), 0, 1))


def place_kernel(order, *refs):
    out = refs[-1]
    half = refs[0].shape[0] - 1
    for n, message in enumerate(refs[:-1]):

        def write(y, rows):
            at = pl.multiple_of((2 * order[n // 2] + n % 2) * half + y, 8)
            out[:, pl.ds(at, 8), :] = rows

        place_rows(message, write)


def finish_kernel(order, lower, upper, _, out, rows, sem):
    half = lower.shape[0] - 1
    for n, message in enumerate((lower, upper)):

        def write(y, block):
            rows[:, n * half + y : n * half + y + 8, :] = block

        place_rows(message, write)
    at = pl.multiple_of(order[3] * 2 * half, 8)
    copy = pltpu.make_async_copy(rows, out.at[:, pl.ds(at, 2 * half), :], sem)
    copy.start()
    copy.wait()


VMEM = pl.BlockSpec(memory_space=pltpu.VMEM)
SMEM = pl.BlockSpec(memory_space=pltpu.SMEM)
ANY = pl.BlockSpec(memory_space=pl.ANY)


def call(kernel, out_shape, scratch, flops, *operands, scalars=0, space=VMEM, limit=36 << 20):
    size = sum(a.size * a.dtype.itemsize for a in operands)
    return pl.pallas_call(
        kernel,
        out_shape=out_shape,
        in_specs=[SMEM] * scalars + [space] * (len(operands) - scalars),
        out_specs=jax.tree.map(lambda _: space, out_shape),
        scratch_shapes=scratch,
        compiler_params=pltpu.CompilerParams(vmem_limit_bytes=limit),
        cost_estimate=pl.CostEstimate(flops=flops, bytes_accessed=size, transcendentals=0),
    )(*operands)


def halves(a, axis):
    high = lax.reduce_precision(a, 8, 7)
    return jnp.concatenate([high, a - high], axis=axis).astype(BF16)


def banded(taps, rows, cols, shift):
    offset = jnp.arange(rows)[:, None] - jnp.arange(cols)[None, :] + shift
    select = (offset[None] == jnp.arange(TAPS)[:, None, None]).astype(F32)
    return jnp.einsum("vt,trc->vrc", taps, select, precision=lax.Precision.HIGHEST)


def swap_near(a, axis):
    return lax.ppermute(a, axis, [(i, i ^ 1) for i in range(lax.axis_size(axis))])


def swap_far(a, axis, ring=False):
    count = lax.axis_size(axis)
    pairs = [(i, i + 1) for i in range(1, count - 1, 2)] + ([(count - 1, 0)] if ring else [])
    return lax.ppermute(a, axis, pairs + [(j, i) for i, j in pairs])


def per_device(estimate, view_data, psf_taps, routes):
    bricks, groups = lax.axis_size("brick"), lax.axis_size("view")
    brick, group = lax.axis_index("brick"), lax.axis_index("view")
    planes, size_y, size_z = estimate.shape
    views_dev, slots = view_data.shape[:2]
    capacity = slots // bricks
    core = size_y // groups
    ext = core + 2 * REACH
    views = views_dev * groups

    place = jnp.stack([group, brick % 2, group % 2])

    def shape(*dims, kind=F32):
        return jax.ShapeDtypeStruct(dims + (size_z,), kind)

    middle, near, far = call(
        prepare_kernel,
        (shape(ext, planes), shape(ext, REACH, kind=BF16), shape(ext, REACH, kind=BF16)),
        [],
        0,
        place,
        estimate,
        scalars=1,
    )
    near, far, psf_taps, routes = lax.optimization_barrier((near, far, psf_taps, routes))
    near, far = swap_near(near, "brick"), swap_far(far, "brick")

    normed = psf_taps / jnp.sum(psf_taps, axis=-1, keepdims=True)
    blocks = routes[..., 0].reshape(views_dev, bricks, planes)
    own = lax.dynamic_index_in_dim(blocks, brick, 1, keepdims=False)
    position = jnp.arange(planes)
    earlier = position[:, None] < position[None, :]
    rank = jnp.sum(((own[:, :, None] == own[:, None, :]) & earlier).astype(jnp.int32), axis=1)
    view_id = jnp.arange(views_dev)[:, None]
    where = ((own * groups + group) * views_dev + view_id) * capacity + rank
    packed = jnp.concatenate(
        [normed.reshape(views_dev, 3 * TAPS), where.astype(F32)], axis=1
    )
    packed = jnp.pad(packed, ((0, 0), (0, 128 - packed.shape[1])))
    across = lax.ppermute(packed, "view", [(i, (i + 2) % groups) for i in range(groups)])
    around = [packed, swap_near(packed, "view"), swap_far(packed, "view", True), across]
    order = jnp.stack([group, group ^ 1, (group + 2 * (group % 2) - 1) % groups, (group + 2) % groups])
    here = order[:, None] == jnp.arange(groups)[None, :]
    packed = jnp.sum(jnp.where(here[:, :, None, None], jnp.stack(around)[:, None], 0.0), axis=0)
    packed = packed.reshape(views, packed.shape[-1])

    sending = call(
        deal_kernel,
        shape(bricks, groups, views_dev, capacity, core, kind=BF16),
        [
            pltpu.VMEM((views_dev * groups, bricks, capacity, core, size_z), BF16),
            pltpu.SemaphoreType.DMA((2, views_dev * groups)),
        ],
        0,
        view_data.reshape(views_dev, bricks, capacity, size_y, size_z),
        space=ANY,
        limit=58 << 20,
    )
    sending = sending.reshape(bricks * groups, views_dev * capacity, core, size_z)
    sending, near, far, packed = lax.optimization_barrier((sending, near, far, packed))
    got = lax.all_to_all(sending, BOTH, 0, 0, tiled=True)
    got = got.reshape(bricks * groups * views_dev * capacity, core, size_z)

    taps = packed[:, : 3 * TAPS].reshape(views, 3, TAPS)
    where = packed[:, 3 * TAPS : 3 * TAPS + planes].astype(jnp.int32).reshape(views * planes)

    mat_x = banded(taps[:, 0], ext, planes, -1)
    mat_y = banded(taps[:, 1], ext, core, -1)
    mat_z = banded(taps[:, 2], size_z, size_z, TAPS // 2)
    ax = halves(mat_x.transpose(0, 2, 1).reshape(views * planes, ext), 1)
    ay = halves(mat_y.transpose(0, 2, 1), 2)
    tz = halves(mat_z, 1)
    axt = halves(mat_x.transpose(1, 0, 2).reshape(ext, views * planes), 0)
    ayt = halves(mat_y, 2)
    tzt = halves(mat_z.transpose(0, 2, 1), 1)

    scratch = pltpu.VMEM((views * planes, ext, size_z), F32)
    wide = pltpu.VMEM((ext, ext, size_z), BF16)
    codes = partial(shape, kind=jnp.int16)
    flops = 4 * 10**9
    rows_shape = (views, planes * core, size_z)
    forward, back = (ax, ay, tz), (axt, ayt, tzt)
    field = (near, middle, far)

    blurred = call(
        blur_kernel,
        jax.ShapeDtypeStruct(rows_shape, BF16),
        [wide, scratch],
        flops,
        place,
        *field,
        *forward,
        scalars=1,
    )
    side = 2 * REACH
    part, nn, fn, nf, ff = call(
        back_kernel,
        (shape(ext, ext),) + (codes(side + 1, side),) * 4,
        [scratch],
        flops,
        place,
        where,
        blurred,
        got,
        *back,
        scalars=2,
    )
    parts = swap_near(nn, "brick"), swap_far(fn, "brick")
    others = swap_near(nf, "brick"), swap_far(ff, "brick")
    half_shape = (shape(side, ext), codes(side + 1, ext))
    total_near, send_near = call(
        partial(gather_half_kernel, 0), half_shape, [], 0, place, part, *parts, scalars=1
    )
    total_far, send_far = call(
        partial(gather_half_kernel, 1), half_shape, [], 0, place, part, *others, scalars=1
    )
    side = REACH
    kept, part, send_near, send_far = call(
        full_kernel,
        (shape(ext, planes), shape(ext, ext), codes(ext + 1, side), codes(ext + 1, side)),
        [wide, scratch, pltpu.VMEM(rows_shape, BF16)],
        2 * flops,
        place,
        where,
        *field,
        total_near,
        total_far,
        swap_near(send_near, "view"),
        swap_far(send_far, "view"),
        got,
        *forward,
        *back,
        scalars=2,
    )
    total, send_near, send_far = call(
        gather_all_kernel,
        (shape(ext, planes), codes(side + 1, planes), codes(side + 1, planes)),
        [],
        0,
        place,
        part,
        swap_near(send_near, "brick"),
        swap_far(send_far, "brick"),
        scalars=1,
    )
    lower, upper = call(
        last_kernel,
        (codes(core // 2 + 1, planes),) * 2,
        [pltpu.VMEM((core, planes, size_z), F32)],
        0,
        place,
        kept,
        total,
        swap_near(send_near, "view"),
        swap_far(send_far, "view"),
        scalars=1,
    )
    lower_far, upper_near = swap_far(lower, "view", True), swap_near(upper, "view")
    upper_far, lower_near = swap_far(upper, "view", True), swap_near(lower, "view")
    lower_last, upper_last = swap_near(lower_far, "view"), swap_far(upper_near, "view", True)
    merged = call(
        place_kernel,
        shape(planes, size_y),
        [],
        0,
        order,
        lower,
        upper,
        lower_near,
        upper_near,
        lower_far,
        upper_far,
        scalars=1,
    )
    return pl.pallas_call(
        finish_kernel,
        out_shape=shape(planes, size_y),
        in_specs=[SMEM, VMEM, VMEM, ANY],
        out_specs=ANY,
        scratch_shapes=[pltpu.VMEM((planes, core, size_z), F32), pltpu.SemaphoreType.DMA],
        input_output_aliases={3: 0},
        compiler_params=pltpu.CompilerParams(vmem_limit_bytes=58 << 20),
    )(order, lower_last, upper_last, merged)


def solution(mesh):
    return jax.shard_map(
        per_device,
        mesh=mesh,
        in_specs=(
            P("brick", None, None),
            P("view", "brick", None, None),
            P("view", None, None),
            P("view", None, None),
        ),
        out_specs=P("brick", None, None),
        check_vma=False,
    )
```

```python
from functools import partial

import jax
import jax.numpy as jnp
from jax import lax
from jax.experimental import pallas as pl
from jax.experimental.pallas import tpu as pltpu
from jax.sharding import PartitionSpec as P

VIEWS = 8
ITERS = 2
TAPS = 31
REACH = 16
BF16 = jnp.bfloat16
F32 = jnp.float32

BOTH = ("brick", "view")


def dot(a, b):
    return jnp.dot(a, b, preferred_element_type=F32)


def twice(a, axis):
    return jnp.concatenate([a, a], axis=axis)


def split(a):
    high = a.astype(BF16)
    return high, (a - high.astype(F32)).astype(BF16)


def blur_steps(fe, ax, ay, tz, t1, views, core, finish):
    ext_y = fe.shape[0]

    def along_x(step, carry):
        y0 = pl.multiple_of(step * 8, 8)
        rows = []
        for k in range(0, 8, 2):
            pair = jnp.concatenate([fe[y0 + k], fe[y0 + k + 1]], axis=1)
            out = dot(ax[...], twice(pair, 0))
            rows += [out[:, :128], out[:, 128:]]
        t1[:, pl.ds(y0, 8), :] = jnp.swapaxes(jnp.stack(rows), 0, 1)
        return carry

    lax.fori_loop(0, ext_y // 8, along_x, 0, unroll=True)

    def along_yz(v, carry):
        rows = []
        for i in range(0, core, 2):
            pair = jnp.concatenate([t1[v * core + i], t1[v * core + i + 1]], axis=1).astype(BF16)
            out = dot(ay[v], twice(pair, 0)).astype(BF16)
            rows += [out[:, :128], out[:, 128:]]
        plane = jnp.concatenate(rows, axis=0)
        finish(v, dot(twice(plane, 1), tz[v]))
        return carry

    lax.fori_loop(0, views, along_yz, 0, unroll=True)


def back_steps(ratio_of, axt, ayt, tzt, t1, out, views, core):
    def along_zy(v, carry):
        high, low = split(dot(twice(ratio_of(v), 1), tzt[v]))
        weights = twice(ayt[v], 1)
        for i in range(0, core, 2):
            here, there = slice(i * core, (i + 1) * core), slice((i + 1) * core, (i + 2) * core)
            pair = jnp.concatenate([high[here], high[there]], axis=1)
            rest = jnp.concatenate([low[here], low[there]], axis=1)
            rows = dot(weights, jnp.concatenate([pair, pair, rest, rest], axis=0))
            t1[v * core + i] = rows[:, :128]
            t1[v * core + i + 1] = rows[:, 128:]
        return carry

    lax.fori_loop(0, views, along_zy, 0, unroll=True)
    ext = out.shape[1]

    def along_x(step, carry):
        y0 = pl.multiple_of(step * 8, 8)
        high, low = split(jnp.swapaxes(t1[:, pl.ds(y0, 8), :], 0, 1))
        for k in range(0, 8, 2):
            both = dot(axt[...], jnp.concatenate([high[k], high[k + 1]], axis=1))
            rest = dot(axt[:ext], jnp.concatenate([low[k], low[k + 1]], axis=1))
            rows = both[:ext] + both[ext:] + rest
            out[y0 + k] = rows[:, :128]
            out[y0 + k + 1] = rows[:, 128:]
        return carry

    lax.fori_loop(0, out.shape[0] // 8, along_x, 0, unroll=True)


SHIFT = 256.0
LEVELS = 65534.0
HALF = 32767


def mark_of(part):
    top = jnp.max(jnp.max(part, axis=0), axis=0, keepdims=True)
    top = jnp.broadcast_to(jnp.max(top, axis=1, keepdims=True), (1, part.shape[-1]))
    return jnp.clip(jnp.ceil(jnp.log2(top)), -100.0, 120.0) + SHIFT


def encode(part, scale):
    return ((part * scale + 0.5).astype(jnp.int32) - HALF).astype(jnp.int16)


def decode(codes, scale):
    return (codes.astype(jnp.int32) + HALF).astype(F32) * scale


def scale_of(message):
    mark = message[message.shape[0] - 1, :16].astype(jnp.int32).astype(F32)[:1]
    return jnp.where(mark > 0, jnp.exp2(mark - SHIFT) / LEVELS, 0.0)


def in_blocks(count, body):
    def step(n, carry):
        body(pl.multiple_of(n * 8, 8))
        return carry

    lax.fori_loop(0, count // 8, step, 0)


def send_part(part, *messages):
    mark = mark_of(part[...])
    scale = jnp.exp2(SHIFT - mark) * LEVELS
    for out, y0, x0 in messages:
        count, width = out.shape[0] - 1, out.shape[1]

        def block(y):
            out[pl.ds(y, 8)] = encode(part[pl.ds(y0 + y, 8), x0 : x0 + width], scale)

        in_blocks(count, block)
        out[count] = jnp.broadcast_to(mark.astype(jnp.int32), out.shape[1:]).astype(jnp.int16)


def sides(odd, last):
    return (1 - odd) * last, odd * last


def odd_of(axis):
    return lax.rem(lax.axis_index(axis), 2)


def for_parity(odd, body):
    for value in (0, 1):
        pl.when(odd == value)(partial(body, value))


def prepare_kernel(estimate, middle, near, far):
    planes, size_y = estimate.shape[:2]
    count = middle.shape[0]
    first = lax.axis_index("view") * (count - 2 * REACH) - REACH
    for y in range(0, count, 8):
        at = first + y
        inside = jnp.logical_and(at >= 0, at < size_y)
        rows = estimate[:, pl.ds(pl.multiple_of(jnp.clip(at, 0, size_y - 8), 8), 8), :]
        middle[y : y + 8] = jnp.where(inside, jnp.swapaxes(rows, 0, 1), 0.0)

    def send(odd):
        x_near, x_far = sides(odd, planes - REACH)
        near[...] = middle[:, x_near : x_near + REACH].astype(BF16)
        far[...] = middle[:, x_far : x_far + REACH].astype(BF16)

    for_parity(odd_of("brick"), send)


def deal_kernel(data, out, stage, sems):
    views, groups, core = data.shape[0], out.shape[1], out.shape[4]
    parts = [(v, q) for v in range(views) for q in range(groups)]
    loads, stores = [], []
    for n, (v, q) in enumerate(parts):
        rows = data.at[v, :, :, q * core : (q + 1) * core, :]
        loads.append(pltpu.make_async_copy(rows, stage.at[n], sems.at[0, n]))
        stores.append(pltpu.make_async_copy(stage.at[n], out.at[:, q, v], sems.at[1, n]))
    for load in loads:
        load.start()
    for load, store in zip(loads, stores):
        load.wait()
        store.start()
    for store in stores:
        store.wait()


def blur_kernel(near, middle, far, ax, ay, tz, out, fe, t1):
    views, core = ay.shape[0], ay.shape[1]

    def join(odd):
        x_near, x_far = sides(odd, REACH + core)
        fe[:, x_near : x_near + REACH] = near[...]
        fe[:, REACH : REACH + core] = middle[...].astype(BF16)
        fe[:, x_far : x_far + REACH] = far[...]

    for_parity(odd_of("brick"), join)

    def finish(v, rows):
        out[v] = rows.astype(BF16)

    blur_steps(fe, ax, ay, tz, t1, views, core, finish)


def ratio_rows(v, core, where, got, den):
    rows = [got[where[v * core + x]] for x in range(core)]
    data = jnp.concatenate(rows, axis=0).astype(F32)
    return (data / den.astype(F32)).astype(BF16)


def back_kernel(where, blurred, got, axt, ayt, tzt, out, nn, fn, nf, ff, t1):
    views, core = ayt.shape[0], got.shape[1]
    back_steps(
        lambda v: ratio_rows(v, core, where, got, blurred[v]), axt, ayt, tzt, t1, out, views, core
    )
    y_near, y_far = sides(odd_of("view"), out.shape[0] // 2)

    def send(odd):
        x_near, x_far = sides(odd, out.shape[1] - nn.shape[1])
        send_part(
            out, (nn, y_near, x_near), (fn, y_near, x_far), (nf, y_far, x_near), (ff, y_far, x_far)
        )

    for_parity(odd_of("brick"), send)


def full_kernel(
    where, near, middle, far, total_near, total_far, got_near, got_far,
    got, ax, ay, tz, axt, ayt, tzt, kept, out, send_near, send_far, fe, t1, ratios,
):
    views, core = ay.shape[0], ay.shape[1]
    y_near, y_far = sides(odd_of("view"), out.shape[0] // 2)

    def renew(odd):
        x_near, x_far = sides(odd, REACH + core)
        fields = (near, x_near, REACH), (far, x_far, REACH), (middle, REACH, core)
        for codes, total, first in ((got_near, total_near, y_near), (got_far, total_far, y_far)):
            scale = scale_of(codes)

            def block(y):
                rows, here = pl.ds(first + y, 8), pl.ds(y, 8)
                for field, x, width in fields:
                    cells = slice(x, x + width)
                    step = (total[here, cells] + decode(codes[here, cells], scale)) / views
                    fresh = field[rows].astype(F32) * step
                    fe[rows, cells] = fresh.astype(BF16)
                    if field is middle:
                        kept[rows] = fresh

            in_blocks(total.shape[0], block)

    for_parity(odd_of("brick"), renew)

    def finish(v, rows):
        ratios[v] = ratio_rows(v, core, where, got, rows.astype(BF16))

    blur_steps(fe, ax, ay, tz, t1, views, core, finish)
    back_steps(lambda v: ratios[v], axt, ayt, tzt, t1, out, views, core)

    def send(odd):
        x_near, x_far = sides(odd, out.shape[1] - REACH)
        send_part(out, (send_near, 0, x_near), (send_far, 0, x_far))

    for_parity(odd_of("brick"), send)


def gather_rows(first, part, near, far, out):
    side = near.shape[1]
    off = (part.shape[1] - 2 * side) // 2
    scale_n, scale_f = scale_of(near), scale_of(far)

    def add_both(odd):
        x_near, x_far = sides(odd, side)

        def block(y):
            rows = pl.ds(y, 8)
            for got, scale, x in ((near, scale_n, x_near), (far, scale_f, x_far)):
                here = part[pl.ds(first + y, 8), off + x : off + x + side]
                out[rows, x : x + side] = here + decode(got[rows], scale)

        in_blocks(out.shape[0], block)

    for_parity(odd_of("brick"), add_both)


def gather_half_kernel(which, part, near, far, out, message):
    first = sides(odd_of("view"), part.shape[0] // 2)[which]
    gather_rows(first, part, near, far, out)
    send_part(out, (message, 0, 0))


def gather_all_kernel(part, near, far, out, send_near, send_far):
    gather_rows(0, part, near, far, out)
    y_near, y_far = sides(odd_of("view"), part.shape[0] - REACH)
    send_part(out, (send_near, y_near, 0), (send_far, y_far, 0))


def last_kernel(field, total, near, far, codes_lo, codes_hi, fresh):
    y_near, y_far = sides(odd_of("view"), REACH)
    for got, first in ((near, y_near), (far, y_far)):
        scale = scale_of(got)

        def block(y):
            rows = pl.ds(REACH + first + y, 8)
            step = (total[rows] + decode(got[pl.ds(y, 8)], scale)) / VIEWS
            fresh[pl.ds(first + y, 8)] = field[rows] * step

        in_blocks(REACH, block)
    send_part(fresh, (codes_lo, 0, 0), (codes_hi, fresh.shape[0] // 2, 0))


def place_rows(message, write):
    scale = scale_of(message)
    for y in range(0, message.shape[0] - 1, 8):
        write(y, jnp.swapaxes(decode(message[y : y + 8], scale), 0, 1))


def groups_around(group, count):
    far = lax.rem(group + 2 * lax.rem(group, 2) - 1 + count, count)
    return group, group + 1 - 2 * lax.rem(group, 2), far, lax.rem(group + 2, count)


def place_kernel(groups, *refs):
    order = groups_around(lax.axis_index("view"), groups)
    out = refs[-1]
    half = refs[0].shape[0] - 1
    for n, message in enumerate(refs[:-1]):

        def write(y, rows):
            at = pl.multiple_of((2 * order[n // 2] + n % 2) * half + y, 8)
            out[:, pl.ds(at, 8), :] = rows

        place_rows(message, write)


def finish_kernel(groups, lower, upper, _, out, rows, sem):
    order = groups_around(lax.axis_index("view"), groups)
    half = lower.shape[0] - 1
    copies = []
    for n, message in enumerate((lower, upper)):

        def write(y, block):
            rows[:, n * half + y : n * half + y + 8, :] = block

        place_rows(message, write)
        at = pl.multiple_of((order[3] * 2 + n) * half, 8)
        part = rows.at[:, n * half : (n + 1) * half, :]
        copies.append(pltpu.make_async_copy(part, out.at[:, pl.ds(at, half), :], sem.at[n]))
        copies[n].start()
    for copy in copies:
        copy.wait()


VMEM = pl.BlockSpec(memory_space=pltpu.VMEM)
SMEM = pl.BlockSpec(memory_space=pltpu.SMEM)
ANY = pl.BlockSpec(memory_space=pl.ANY)


def call(kernel, out_shape, scratch, flops, *operands, scalars=0, space=VMEM, limit=36 << 20):
    size = sum(a.size * a.dtype.itemsize for a in operands)
    return pl.pallas_call(
        kernel,
        out_shape=out_shape,
        in_specs=[SMEM] * scalars + [space] * (len(operands) - scalars),
        out_specs=jax.tree.map(lambda _: space, out_shape),
        scratch_shapes=scratch,
        compiler_params=pltpu.CompilerParams(vmem_limit_bytes=limit),
        cost_estimate=pl.CostEstimate(flops=flops, bytes_accessed=size, transcendentals=0),
    )(*operands)


def halves(a, axis):
    high = lax.reduce_precision(a, 8, 7)
    return jnp.concatenate([high, a - high], axis=axis).astype(BF16)


def banded(taps, rows, cols, shift):
    offset = jnp.arange(rows)[:, None] - jnp.arange(cols)[None, :] + shift
    select = (offset[None] == jnp.arange(TAPS)[:, None, None]).astype(F32)
    return jnp.einsum("vt,trc->vrc", taps, select, precision=lax.Precision.HIGHEST)


def swap_near(a, axis):
    return lax.ppermute(a, axis, [(i, i ^ 1) for i in range(lax.axis_size(axis))])


def swap_far(a, axis, ring=False):
    count = lax.axis_size(axis)
    pairs = [(i, i + 1) for i in range(1, count - 1, 2)] + ([(count - 1, 0)] if ring else [])
    return lax.ppermute(a, axis, pairs + [(j, i) for i, j in pairs])


def per_device(estimate, view_data, psf_taps, routes):
    bricks, groups = lax.axis_size("brick"), lax.axis_size("view")
    brick, group = lax.axis_index("brick"), lax.axis_index("view")
    planes, size_y, size_z = estimate.shape
    views_dev, slots = view_data.shape[:2]
    capacity = slots // bricks
    core = size_y // groups
    ext = core + 2 * REACH
    views = views_dev * groups

    def shape(*dims, kind=F32):
        return jax.ShapeDtypeStruct(dims + (size_z,), kind)

    middle, near, far = call(
        prepare_kernel,
        (shape(ext, planes), shape(ext, REACH, kind=BF16), shape(ext, REACH, kind=BF16)),
        [],
        0,
        estimate,
    )
    near, far, psf_taps, routes = lax.optimization_barrier((near, far, psf_taps, routes))
    near, far = swap_near(near, "brick"), swap_far(far, "brick")

    normed = psf_taps / jnp.sum(psf_taps, axis=-1, keepdims=True)
    blocks = routes[..., 0].reshape(views_dev, bricks, planes)
    own = lax.dynamic_index_in_dim(blocks, brick, 1, keepdims=False)
    position = jnp.arange(planes)
    earlier = position[:, None] < position[None, :]
    rank = jnp.sum(((own[:, :, None] == own[:, None, :]) & earlier).astype(jnp.int32), axis=1)
    view_id = jnp.arange(views_dev)[:, None]
    where = ((own * groups + group) * views_dev + view_id) * capacity + rank
    packed = jnp.concatenate(
        [normed.reshape(views_dev, 3 * TAPS), where.astype(F32)], axis=1
    )
    packed = jnp.pad(packed, ((0, 0), (0, 128 - packed.shape[1])))
    across = lax.ppermute(packed, "view", [(i, (i + 2) % groups) for i in range(groups)])
    around = [packed, swap_near(packed, "view"), swap_far(packed, "view", True), across]
    order = jnp.stack([group, group ^ 1, (group + 2 * (group % 2) - 1) % groups, (group + 2) % groups])
    here = order[:, None] == jnp.arange(groups)[None, :]
    packed = jnp.sum(jnp.where(here[:, :, None, None], jnp.stack(around)[:, None], 0.0), axis=0)
    packed = packed.reshape(views, packed.shape[-1])

    sending = call(
        deal_kernel,
        shape(bricks, groups, views_dev, capacity, core, kind=BF16),
        [
            pltpu.VMEM((views_dev * groups, bricks, capacity, core, size_z), BF16),
            pltpu.SemaphoreType.DMA((2, views_dev * groups)),
        ],
        0,
        view_data.reshape(views_dev, bricks, capacity, size_y, size_z),
        space=ANY,
        limit=58 << 20,
    )
    sending = sending.reshape(bricks * groups, views_dev * capacity, core, size_z)
    sending, near, far, packed = lax.optimization_barrier((sending, near, far, packed))
    got = lax.all_to_all(sending, BOTH, 0, 0, tiled=True)
    got = got.reshape(bricks * groups * views_dev * capacity, core, size_z)

    taps = packed[:, : 3 * TAPS].reshape(views, 3, TAPS)
    where = packed[:, 3 * TAPS : 3 * TAPS + planes].astype(jnp.int32).reshape(views * planes)

    mat_x = banded(taps[:, 0], ext, planes, -1)
    mat_y = banded(taps[:, 1], ext, core, -1)
    mat_z = banded(taps[:, 2], size_z, size_z, TAPS // 2)
    ax = halves(mat_x.transpose(0, 2, 1).reshape(views * planes, ext), 1)
    ay = halves(mat_y.transpose(0, 2, 1), 2)
    tz = halves(mat_z, 1)
    axt = halves(mat_x.transpose(1, 0, 2).reshape(ext, views * planes), 0)
    ayt = halves(mat_y, 2)
    tzt = halves(mat_z.transpose(0, 2, 1), 1)

    scratch = pltpu.VMEM((views * planes, ext, size_z), F32)
    wide = pltpu.VMEM((ext, ext, size_z), BF16)
    codes = partial(shape, kind=jnp.int16)
    flops = 4 * 10**9
    rows_shape = (views, planes * core, size_z)
    forward, back = (ax, ay, tz), (axt, ayt, tzt)
    field = (near, middle, far)

    blurred = call(
        blur_kernel,
        jax.ShapeDtypeStruct(rows_shape, BF16),
        [wide, scratch],
        flops,
        *field,
        *forward,
    )
    side = 2 * REACH
    part, nn, fn, nf, ff = call(
        back_kernel,
        (shape(ext, ext),) + (codes(side + 1, side),) * 4,
        [scratch],
        flops,
        where,
        blurred,
        got,
        *back,
        scalars=1,
    )
    parts = swap_near(nn, "brick"), swap_far(fn, "brick")
    others = swap_near(nf, "brick"), swap_far(ff, "brick")
    half_shape = (shape(side, ext), codes(side + 1, ext))
    total_near, send_near = call(
        partial(gather_half_kernel, 0), half_shape, [], 0, part, *parts
    )
    total_far, send_far = call(
        partial(gather_half_kernel, 1), half_shape, [], 0, part, *others
    )
    side = REACH
    kept, part, send_near, send_far = call(
        full_kernel,
        (shape(ext, planes), shape(ext, ext), codes(ext + 1, side), codes(ext + 1, side)),
        [wide, scratch, pltpu.VMEM(rows_shape, BF16)],
        2 * flops,
        where,
        *field,
        total_near,
        total_far,
        swap_near(send_near, "view"),
        swap_far(send_far, "view"),
        got,
        *forward,
        *back,
        scalars=1,
    )
    total, send_near, send_far = call(
        gather_all_kernel,
        (shape(ext, planes), codes(side + 1, planes), codes(side + 1, planes)),
        [],
        0,
        part,
        swap_near(send_near, "brick"),
        swap_far(send_far, "brick"),
    )
    lower, upper = call(
        last_kernel,
        (codes(core // 2 + 1, planes),) * 2,
        [pltpu.VMEM((core, planes, size_z), F32)],
        0,
        kept,
        total,
        swap_near(send_near, "view"),
        swap_far(send_far, "view"),
    )
    lower_far, upper_near = swap_far(lower, "view", True), swap_near(upper, "view")
    upper_far, lower_near = swap_far(upper, "view", True), swap_near(lower, "view")
    lower_last, upper_last = swap_near(lower_far, "view"), swap_far(upper_near, "view", True)
    merged = call(
        partial(place_kernel, groups),
        shape(planes, size_y),
        [],
        0,
        lower,
        upper,
        lower_near,
        upper_near,
        lower_far,
        upper_far,
    )
    return pl.pallas_call(
        partial(finish_kernel, groups),
        out_shape=shape(planes, size_y),
        in_specs=[VMEM, VMEM, ANY],
        out_specs=ANY,
        scratch_shapes=[pltpu.VMEM((planes, core, size_z), F32), pltpu.SemaphoreType.DMA((2,))],
        input_output_aliases={2: 0},
        compiler_params=pltpu.CompilerParams(vmem_limit_bytes=36 << 20),
    )(lower_last, upper_last, merged)


def solution(mesh):
    return jax.shard_map(
        per_device,
        mesh=mesh,
        in_specs=(
            P("brick", None, None),
            P("view", "brick", None, None),
            P("view", None, None),
            P("view", None, None),
        ),
        out_specs=P("brick", None, None),
        check_vma=False,
    )
```

```python
from functools import partial

import jax
import jax.numpy as jnp
from jax import lax
from jax.experimental import pallas as pl
from jax.experimental.pallas import tpu as pltpu
from jax.sharding import PartitionSpec as P

VIEWS = 8
ITERS = 2
TAPS = 31
REACH = 16
BF16 = jnp.bfloat16
F32 = jnp.float32

BOTH = ("brick", "view")


def dot(a, b):
    return jnp.dot(a, b, preferred_element_type=F32)


def twice(a, axis):
    return jnp.concatenate([a, a], axis=axis)


def split(a):
    high = a.astype(BF16)
    return high, (a - high.astype(F32)).astype(BF16)


def blur_steps(fe, ax, ay, tz, t1, views, core, finish):
    ext_y = fe.shape[0]

    def along_x(step, carry):
        y0 = pl.multiple_of(step * 8, 8)
        rows = []
        for k in range(0, 8, 2):
            pair = jnp.concatenate([fe[y0 + k], fe[y0 + k + 1]], axis=1)
            out = dot(ax[...], twice(pair, 0))
            rows += [out[:, :128], out[:, 128:]]
        t1[:, pl.ds(y0, 8), :] = jnp.swapaxes(jnp.stack(rows), 0, 1)
        return carry

    lax.fori_loop(0, ext_y // 8, along_x, 0, unroll=True)

    def along_yz(v, carry):
        rows = []
        for i in range(0, core, 2):
            pair = jnp.concatenate([t1[v * core + i], t1[v * core + i + 1]], axis=1).astype(BF16)
            out = dot(ay[v], twice(pair, 0)).astype(BF16)
            rows += [out[:, :128], out[:, 128:]]
        plane = jnp.concatenate(rows, axis=0)
        finish(v, dot(twice(plane, 1), tz[v]))
        return carry

    lax.fori_loop(0, views, along_yz, 0, unroll=True)


def back_steps(ratio_of, axt, ayt, tzt, t1, out, views, core):
    def along_zy(v, carry):
        high, low = split(dot(twice(ratio_of(v), 1), tzt[v]))
        weights = twice(ayt[v], 1)
        for i in range(0, core, 2):
            here, there = slice(i * core, (i + 1) * core), slice((i + 1) * core, (i + 2) * core)
            pair = jnp.concatenate([high[here], high[there]], axis=1)
            rest = jnp.concatenate([low[here], low[there]], axis=1)
            rows = dot(weights, jnp.concatenate([pair, pair, rest, rest], axis=0))
            t1[v * core + i] = rows[:, :128]
            t1[v * core + i + 1] = rows[:, 128:]
        return carry

    lax.fori_loop(0, views, along_zy, 0, unroll=True)
    ext = out.shape[1]

    def along_x(step, carry):
        y0 = pl.multiple_of(step * 8, 8)
        high, low = split(jnp.swapaxes(t1[:, pl.ds(y0, 8), :], 0, 1))
        for k in range(0, 8, 2):
            both = dot(axt[...], jnp.concatenate([high[k], high[k + 1]], axis=1))
            rest = dot(axt[:ext], jnp.concatenate([low[k], low[k + 1]], axis=1))
            rows = both[:ext] + both[ext:] + rest
            out[y0 + k] = rows[:, :128]
            out[y0 + k + 1] = rows[:, 128:]
        return carry

    lax.fori_loop(0, out.shape[0] // 8, along_x, 0, unroll=True)


SHIFT = 256.0
LEVELS = 65534.0
HALF = 32767


def mark_of(part):
    top = jnp.max(jnp.max(part, axis=0), axis=0, keepdims=True)
    top = jnp.broadcast_to(jnp.max(top, axis=1, keepdims=True), (1, part.shape[-1]))
    return jnp.clip(jnp.ceil(jnp.log2(top)), -100.0, 120.0) + SHIFT


def encode(part, scale):
    return ((part * scale + 0.5).astype(jnp.int32) - HALF).astype(jnp.int16)


def decode(codes, scale):
    return (codes.astype(jnp.int32) + HALF).astype(F32) * scale


def scale_of(message):
    mark = message[message.shape[0] - 1, :16].astype(jnp.int32).astype(F32)[:1]
    return jnp.where(mark > 0, jnp.exp2(mark - SHIFT) / LEVELS, 0.0)


def in_blocks(count, body):
    def step(n, carry):
        body(pl.multiple_of(n * 8, 8))
        return carry

    lax.fori_loop(0, count // 8, step, 0)


def send_part(part, *messages):
    mark = mark_of(part[...])
    scale = jnp.exp2(SHIFT - mark) * LEVELS
    for out, y0, x0 in messages:
        count, width = out.shape[0] - 1, out.shape[1]

        def block(y):
            out[pl.ds(y, 8)] = encode(part[pl.ds(y0 + y, 8), x0 : x0 + width], scale)

        in_blocks(count, block)
        out[count] = jnp.broadcast_to(mark.astype(jnp.int32), out.shape[1:]).astype(jnp.int16)


def sides(odd, last):
    return (1 - odd) * last, odd * last


def odd_of(axis):
    return lax.rem(lax.axis_index(axis), 2)


def for_parity(odd, body):
    for value in (0, 1):
        pl.when(odd == value)(partial(body, value))


def send_x(part, near, far):
    def send(odd):
        x_near, x_far = sides(odd, part.shape[1] - near.shape[1])
        send_part(part, (near, 0, x_near), (far, 0, x_far))

    for_parity(odd_of("brick"), send)


def prepare_kernel(estimate, middle, near, far):
    planes, size_y = estimate.shape[:2]
    count = middle.shape[0]
    first = lax.axis_index("view") * (count - 2 * REACH) - REACH
    for y in range(0, count, 8):
        at = first + y
        inside = jnp.logical_and(at >= 0, at < size_y)
        rows = estimate[:, pl.ds(pl.multiple_of(jnp.clip(at, 0, size_y - 8), 8), 8), :]
        middle[y : y + 8] = jnp.where(inside, jnp.swapaxes(rows, 0, 1), 0.0)

    def send(odd):
        x_near, x_far = sides(odd, planes - REACH)
        near[...] = middle[:, x_near : x_near + REACH].astype(BF16)
        far[...] = middle[:, x_far : x_far + REACH].astype(BF16)

    for_parity(odd_of("brick"), send)


def deal_kernel(data, out, stage, sems):
    views, groups, core = data.shape[0], out.shape[1], out.shape[4]
    parts = [(v, q) for v in range(views) for q in range(groups)]
    loads, stores = [], []
    for n, (v, q) in enumerate(parts):
        rows = data.at[v, :, :, q * core : (q + 1) * core, :]
        loads.append(pltpu.make_async_copy(rows, stage.at[n], sems.at[0, n]))
        stores.append(pltpu.make_async_copy(stage.at[n], out.at[:, q, v], sems.at[1, n]))
    for load in loads:
        load.start()
    for load, store in zip(loads, stores):
        load.wait()
        store.start()
    for store in stores:
        store.wait()


def blur_kernel(near, middle, far, ax, ay, tz, out, fe, t1):
    views, core = ay.shape[0], ay.shape[1]

    def join(odd):
        x_near, x_far = sides(odd, REACH + core)
        fe[:, x_near : x_near + REACH] = near[...]
        fe[:, REACH : REACH + core] = middle[...].astype(BF16)
        fe[:, x_far : x_far + REACH] = far[...]

    for_parity(odd_of("brick"), join)

    def finish(v, rows):
        out[v] = rows.astype(BF16)

    blur_steps(fe, ax, ay, tz, t1, views, core, finish)


def ratio_rows(v, core, where, got, den):
    rows = [got[where[v * core + x]] for x in range(core)]
    data = jnp.concatenate(rows, axis=0).astype(F32)
    return (data / den.astype(F32)).astype(BF16)


def back_kernel(where, blurred, got, axt, ayt, tzt, out, send_near, send_far, t1):
    views, core = ayt.shape[0], got.shape[1]
    back_steps(
        lambda v: ratio_rows(v, core, where, got, blurred[v]), axt, ayt, tzt, t1, out, views, core
    )
    send_x(out, send_near, send_far)


def full_kernel(
    where, near, middle, far, total_near, total_far, got_nn, got_nf, got_fn, got_ff,
    got, ax, ay, tz, axt, ayt, tzt, kept, out, send_near, send_far, fe, t1, ratios,
):
    views, core = ay.shape[0], ay.shape[1]
    y_near, y_far = sides(odd_of("view"), out.shape[0] // 2)

    def renew(odd):
        columns = zip(
            sides(odd, core),
            sides(odd, REACH + core),
            (near, far),
            (total_near, total_far),
            ((got_nn, got_nf), (got_fn, got_ff)),
        )
        for start, x_outer, outer, total, messages in columns:
            x_inner = 2 * start + REACH - x_outer
            inner = middle.at[:, x_inner - REACH : x_inner]
            for codes, first in zip(messages, (y_near, y_far)):
                scale = scale_of(codes)

                def block(y):
                    rows, here = pl.ds(first + y, 8), pl.ds(y, 8)
                    for x, field in ((x_outer, outer), (x_inner, inner)):
                        cells = slice(x - start, x - start + REACH)
                        step = (total[rows, cells] + decode(codes[here, cells], scale)) / views
                        fresh = field[rows].astype(F32) * step
                        fe[rows, x : x + REACH] = fresh.astype(BF16)
                        if field is inner:
                            kept[rows, x - REACH : x] = fresh

                in_blocks(codes.shape[0] - 1, block)

    for_parity(odd_of("brick"), renew)

    def finish(v, rows):
        ratios[v] = ratio_rows(v, core, where, got, rows.astype(BF16))

    blur_steps(fe, ax, ay, tz, t1, views, core, finish)
    back_steps(lambda v: ratios[v], axt, ayt, tzt, t1, out, views, core)
    send_x(out, send_near, send_far)


def gather_side_kernel(which, part, got, out, send_near, send_far):
    scale, side = scale_of(got), got.shape[1]

    def add(odd):
        x = sides(odd, side)[which]

        def block(y):
            rows = pl.ds(y, 8)
            out[rows] = part[rows, x : x + side] + decode(got[rows], scale)

        in_blocks(out.shape[0], block)

    for_parity(odd_of("brick"), add)
    y_near, y_far = sides(odd_of("view"), out.shape[0] // 2)
    send_part(out, (send_near, y_near, 0), (send_far, y_far, 0))


def gather_kernel(part, near, far, out, send_near, send_far):
    side = near.shape[1]
    off = (part.shape[1] - 2 * side) // 2
    scale_n, scale_f = scale_of(near), scale_of(far)

    def add_both(odd):
        x_near, x_far = sides(odd, side)

        def block(y):
            rows = pl.ds(y, 8)
            for got, scale, x in ((near, scale_n, x_near), (far, scale_f, x_far)):
                here = part[rows, off + x : off + x + side]
                out[rows, x : x + side] = here + decode(got[rows], scale)

        in_blocks(out.shape[0], block)

    for_parity(odd_of("brick"), add_both)
    y_near, y_far = sides(odd_of("view"), out.shape[0] - send_near.shape[0] + 1)
    send_part(out, (send_near, y_near, 0), (send_far, y_far, 0))


def last_kernel(field, total, near, far, codes_lo, codes_hi, fresh):
    y_near, y_far = sides(odd_of("view"), REACH)
    for got, first in ((near, y_near), (far, y_far)):
        scale = scale_of(got)

        def block(y):
            rows = pl.ds(REACH + first + y, 8)
            step = (total[rows] + decode(got[pl.ds(y, 8)], scale)) / VIEWS
            fresh[pl.ds(first + y, 8)] = field[rows] * step

        in_blocks(REACH, block)
    send_part(fresh, (codes_lo, 0, 0), (codes_hi, fresh.shape[0] // 2, 0))


def place_rows(message, write):
    scale = scale_of(message)
    for y in range(0, message.shape[0] - 1, 8):
        write(y, jnp.swapaxes(decode(message[y : y + 8], scale), 0, 1))


def groups_around(group, count):
    far = lax.rem(group + 2 * lax.rem(group, 2) - 1 + count, count)
    return group, group + 1 - 2 * lax.rem(group, 2), far, lax.rem(group + 2, count)


def place_kernel(groups, *refs):
    order = groups_around(lax.axis_index("view"), groups)
    out = refs[-1]
    half = refs[0].shape[0] - 1
    for n, message in enumerate(refs[:-1]):

        def write(y, rows):
            at = pl.multiple_of((2 * order[n // 2] + n % 2) * half + y, 8)
            out[:, pl.ds(at, 8), :] = rows

        place_rows(message, write)


def finish_kernel(groups, lower, upper, _, out, rows, sem):
    order = groups_around(lax.axis_index("view"), groups)
    half = lower.shape[0] - 1
    copies = []
    for n, message in enumerate((lower, upper)):

        def write(y, block):
            rows[:, n * half + y : n * half + y + 8, :] = block

        place_rows(message, write)
        at = pl.multiple_of((order[3] * 2 + n) * half, 8)
        part = rows.at[:, n * half : (n + 1) * half, :]
        copies.append(pltpu.make_async_copy(part, out.at[:, pl.ds(at, half), :], sem.at[n]))
        copies[n].start()
    for copy in copies:
        copy.wait()


VMEM = pl.BlockSpec(memory_space=pltpu.VMEM)
SMEM = pl.BlockSpec(memory_space=pltpu.SMEM)
ANY = pl.BlockSpec(memory_space=pl.ANY)


def call(kernel, out_shape, scratch, flops, *operands, scalars=0, space=VMEM, limit=36 << 20):
    size = sum(a.size * a.dtype.itemsize for a in operands)
    return pl.pallas_call(
        kernel,
        out_shape=out_shape,
        in_specs=[SMEM] * scalars + [space] * (len(operands) - scalars),
        out_specs=jax.tree.map(lambda _: space, out_shape),
        scratch_shapes=scratch,
        compiler_params=pltpu.CompilerParams(vmem_limit_bytes=limit),
        cost_estimate=pl.CostEstimate(flops=flops, bytes_accessed=size, transcendentals=0),
    )(*operands)


def halves(a, axis):
    high = lax.reduce_precision(a, 8, 7)
    return jnp.concatenate([high, a - high], axis=axis).astype(BF16)


def banded(taps, rows, cols, shift):
    offset = jnp.arange(rows)[:, None] - jnp.arange(cols)[None, :] + shift
    select = (offset[None] == jnp.arange(TAPS)[:, None, None]).astype(F32)
    return jnp.einsum("vt,trc->vrc", taps, select, precision=lax.Precision.HIGHEST)


def swap_near(a, axis):
    return lax.ppermute(a, axis, [(i, i ^ 1) for i in range(lax.axis_size(axis))])


def swap_far(a, axis, ring=False):
    count = lax.axis_size(axis)
    pairs = [(i, i + 1) for i in range(1, count - 1, 2)] + ([(count - 1, 0)] if ring else [])
    return lax.ppermute(a, axis, pairs + [(j, i) for i, j in pairs])


def per_device(estimate, view_data, psf_taps, routes):
    bricks, groups = lax.axis_size("brick"), lax.axis_size("view")
    brick, group = lax.axis_index("brick"), lax.axis_index("view")
    planes, size_y, size_z = estimate.shape
    views_dev, slots = view_data.shape[:2]
    capacity = slots // bricks
    core = size_y // groups
    ext = core + 2 * REACH
    views = views_dev * groups

    def shape(*dims, kind=F32):
        return jax.ShapeDtypeStruct(dims + (size_z,), kind)

    middle, near, far = call(
        prepare_kernel,
        (shape(ext, planes), shape(ext, REACH, kind=BF16), shape(ext, REACH, kind=BF16)),
        [],
        0,
        estimate,
    )
    near, far, psf_taps, routes = lax.optimization_barrier((near, far, psf_taps, routes))
    near, far = swap_near(near, "brick"), swap_far(far, "brick")

    normed = psf_taps / jnp.sum(psf_taps, axis=-1, keepdims=True)
    blocks = routes[..., 0].reshape(views_dev, bricks, planes)
    own = lax.dynamic_index_in_dim(blocks, brick, 1, keepdims=False)
    position = jnp.arange(planes)
    earlier = position[:, None] < position[None, :]
    rank = jnp.sum(((own[:, :, None] == own[:, None, :]) & earlier).astype(jnp.int32), axis=1)
    view_id = jnp.arange(views_dev)[:, None]
    where = ((own * groups + group) * views_dev + view_id) * capacity + rank
    packed = jnp.concatenate(
        [normed.reshape(views_dev, 3 * TAPS), where.astype(F32)], axis=1
    )
    packed = jnp.pad(packed, ((0, 0), (0, 128 - packed.shape[1])))
    across = lax.ppermute(packed, "view", [(i, (i + 2) % groups) for i in range(groups)])
    around = [packed, swap_near(packed, "view"), swap_far(packed, "view", True), across]
    order = jnp.stack([group, group ^ 1, (group + 2 * (group % 2) - 1) % groups, (group + 2) % groups])
    here = order[:, None] == jnp.arange(groups)[None, :]
    packed = jnp.sum(jnp.where(here[:, :, None, None], jnp.stack(around)[:, None], 0.0), axis=0)
    packed = packed.reshape(views, packed.shape[-1])

    sending = call(
        deal_kernel,
        shape(bricks, groups, views_dev, capacity, core, kind=BF16),
        [
            pltpu.VMEM((views_dev * groups, bricks, capacity, core, size_z), BF16),
            pltpu.SemaphoreType.DMA((2, views_dev * groups)),
        ],
        0,
        view_data.reshape(views_dev, bricks, capacity, size_y, size_z),
        space=ANY,
        limit=58 << 20,
    )
    sending = sending.reshape(bricks * groups, views_dev * capacity, core, size_z)
    sending, near, far, packed = lax.optimization_barrier((sending, near, far, packed))
    got = lax.all_to_all(sending, BOTH, 0, 0, tiled=True)
    got = got.reshape(bricks * groups * views_dev * capacity, core, size_z)

    taps = packed[:, : 3 * TAPS].reshape(views, 3, TAPS)
    where = packed[:, 3 * TAPS : 3 * TAPS + planes].astype(jnp.int32).reshape(views * planes)

    mat_x = banded(taps[:, 0], ext, planes, -1)
    mat_y = banded(taps[:, 1], ext, core, -1)
    mat_z = banded(taps[:, 2], size_z, size_z, TAPS // 2)
    ax = halves(mat_x.transpose(0, 2, 1).reshape(views * planes, ext), 1)
    ay = halves(mat_y.transpose(0, 2, 1), 2)
    tz = halves(mat_z, 1)
    axt = halves(mat_x.transpose(1, 0, 2).reshape(ext, views * planes), 0)
    ayt = halves(mat_y, 2)
    tzt = halves(mat_z.transpose(0, 2, 1), 1)

    scratch = pltpu.VMEM((views * planes, ext, size_z), F32)
    wide = pltpu.VMEM((ext, ext, size_z), BF16)
    codes = partial(shape, kind=jnp.int16)
    flops = 4 * 10**9
    rows_shape = (views, planes * core, size_z)
    forward, back = (ax, ay, tz), (axt, ayt, tzt)
    field = (near, middle, far)

    blurred = call(
        blur_kernel,
        jax.ShapeDtypeStruct(rows_shape, BF16),
        [wide, scratch],
        flops,
        *field,
        *forward,
    )
    side = 2 * REACH
    part, send_near, send_far = call(
        back_kernel,
        (shape(ext, ext),) + (codes(ext + 1, side),) * 2,
        [scratch],
        flops,
        where,
        blurred,
        got,
        *back,
        scalars=1,
    )
    side_shape = (shape(ext, side),) + (codes(side + 1, side),) * 2
    from_far, from_near = swap_far(send_far, "brick"), swap_near(send_near, "brick")
    total_near, nn, nf = call(partial(gather_side_kernel, 0), side_shape, [], 0, part, from_near)
    total_far, fn, ff = call(partial(gather_side_kernel, 1), side_shape, [], 0, part, from_far)
    side = REACH
    kept, part, send_near, send_far = call(
        full_kernel,
        (shape(ext, planes), shape(ext, ext), codes(ext + 1, side), codes(ext + 1, side)),
        [wide, scratch, pltpu.VMEM(rows_shape, BF16)],
        2 * flops,
        where,
        *field,
        total_near,
        total_far,
        swap_near(nn, "view"),
        swap_far(nf, "view"),
        swap_near(fn, "view"),
        swap_far(ff, "view"),
        got,
        *forward,
        *back,
        scalars=1,
    )
    total, send_near, send_far = call(
        gather_kernel,
        (shape(ext, planes), codes(side + 1, planes), codes(side + 1, planes)),
        [],
        0,
        part,
        swap_near(send_near, "brick"),
        swap_far(send_far, "brick"),
    )
    lower, upper = call(
        last_kernel,
        (codes(core // 2 + 1, planes),) * 2,
        [pltpu.VMEM((core, planes, size_z), F32)],
        0,
        kept,
        total,
        swap_near(send_near, "view"),
        swap_far(send_far, "view"),
    )
    lower_far, upper_near = swap_far(lower, "view", True), swap_near(upper, "view")
    upper_far, lower_near = swap_far(upper, "view", True), swap_near(lower, "view")
    lower_last, upper_last = swap_near(lower_far, "view"), swap_far(upper_near, "view", True)
    merged = call(
        partial(place_kernel, groups),
        shape(planes, size_y),
        [],
        0,
        lower,
        upper,
        lower_near,
        upper_near,
        lower_far,
        upper_far,
    )
    return pl.pallas_call(
        partial(finish_kernel, groups),
        out_shape=shape(planes, size_y),
        in_specs=[VMEM, VMEM, ANY],
        out_specs=ANY,
        scratch_shapes=[pltpu.VMEM((planes, core, size_z), F32), pltpu.SemaphoreType.DMA((2,))],
        input_output_aliases={2: 0},
        compiler_params=pltpu.CompilerParams(vmem_limit_bytes=36 << 20),
    )(lower_last, upper_last, merged)


def solution(mesh):
    return jax.shard_map(
        per_device,
        mesh=mesh,
        in_specs=(
            P("brick", None, None),
            P("view", "brick", None, None),
            P("view", None, None),
            P("view", None, None),
        ),
        out_specs=P("brick", None, None),
        check_vma=False,
    )
```

```python
from functools import partial

import jax
import jax.numpy as jnp
from jax import lax
from jax.experimental import pallas as pl
from jax.experimental.pallas import tpu as pltpu
from jax.sharding import PartitionSpec as P

VIEWS = 8
ITERS = 2
TAPS = 31
REACH = 16
BF16 = jnp.bfloat16
F32 = jnp.float32

BOTH = ("brick", "view")


def dot(a, b):
    return jnp.dot(a, b, preferred_element_type=F32)


def twice(a, axis):
    return jnp.concatenate([a, a], axis=axis)


def split(a):
    high = a.astype(BF16)
    return high, (a - high.astype(F32)).astype(BF16)


def blur_steps(fe, ax, ay, tz, t1, views, core, finish):
    ext_y = fe.shape[0]

    def along_x(step, carry):
        y0 = pl.multiple_of(step * 8, 8)
        rows = []
        for k in range(0, 8, 2):
            pair = jnp.concatenate([fe[y0 + k], fe[y0 + k + 1]], axis=1)
            out = dot(ax[...], twice(pair, 0))
            rows += [out[:, :128], out[:, 128:]]
        t1[:, pl.ds(y0, 8), :] = jnp.swapaxes(jnp.stack(rows), 0, 1)
        return carry

    lax.fori_loop(0, ext_y // 8, along_x, 0, unroll=True)

    def along_yz(v, carry):
        rows = []
        for i in range(0, core, 2):
            pair = jnp.concatenate([t1[v * core + i], t1[v * core + i + 1]], axis=1).astype(BF16)
            out = dot(ay[v], twice(pair, 0)).astype(BF16)
            rows += [out[:, :128], out[:, 128:]]
        plane = jnp.concatenate(rows, axis=0)
        finish(v, dot(twice(plane, 1), tz[v]))
        return carry

    lax.fori_loop(0, views, along_yz, 0, unroll=True)


def back_steps(ratio_of, axt, ayt, tzt, t1, out, views, core):
    def along_zy(v, carry):
        high, low = split(dot(twice(ratio_of(v), 1), tzt[v]))
        weights = twice(ayt[v], 1)
        for i in range(0, core, 2):
            here, there = slice(i * core, (i + 1) * core), slice((i + 1) * core, (i + 2) * core)
            pair = jnp.concatenate([high[here], high[there]], axis=1)
            rest = jnp.concatenate([low[here], low[there]], axis=1)
            rows = dot(weights, jnp.concatenate([pair, pair, rest, rest], axis=0))
            t1[v * core + i] = rows[:, :128]
            t1[v * core + i + 1] = rows[:, 128:]
        return carry

    lax.fori_loop(0, views, along_zy, 0, unroll=True)
    ext = out.shape[1]

    def along_x(step, carry):
        y0 = pl.multiple_of(step * 8, 8)
        high, low = split(jnp.swapaxes(t1[:, pl.ds(y0, 8), :], 0, 1))
        for k in range(0, 8, 2):
            both = dot(axt[...], jnp.concatenate([high[k], high[k + 1]], axis=1))
            rest = dot(axt[:ext], jnp.concatenate([low[k], low[k + 1]], axis=1))
            rows = both[:ext] + both[ext:] + rest
            out[y0 + k] = rows[:, :128]
            out[y0 + k + 1] = rows[:, 128:]
        return carry

    lax.fori_loop(0, out.shape[0] // 8, along_x, 0, unroll=True)


SHIFT = 256.0
LEVELS = 65534.0
HALF = 32767


def mark_of(part):
    top = jnp.max(jnp.max(part, axis=0), axis=0, keepdims=True)
    top = jnp.broadcast_to(jnp.max(top, axis=1, keepdims=True), (1, part.shape[-1]))
    return jnp.clip(jnp.ceil(jnp.log2(top)), -100.0, 120.0) + SHIFT


def encode(part, scale):
    return ((part * scale + 0.5).astype(jnp.int32) - HALF).astype(jnp.int16)


def decode(codes, scale):
    return (codes.astype(jnp.int32) + HALF).astype(F32) * scale


def scale_of(message):
    mark = message[message.shape[0] - 1, :16].astype(jnp.int32).astype(F32)[:1]
    return jnp.where(mark > 0, jnp.exp2(mark - SHIFT) / LEVELS, 0.0)


def in_blocks(count, body):
    def step(n, carry):
        body(pl.multiple_of(n * 8, 8))
        return carry

    lax.fori_loop(0, count // 8, step, 0)


def send_part(part, *messages):
    mark = mark_of(part[...])
    scale = jnp.exp2(SHIFT - mark) * LEVELS
    for out, y0, x0 in messages:
        count, width = out.shape[0] - 1, out.shape[1]

        def block(y):
            out[pl.ds(y, 8)] = encode(part[pl.ds(y0 + y, 8), x0 : x0 + width], scale)

        in_blocks(count, block)
        out[count] = jnp.broadcast_to(mark.astype(jnp.int32), out.shape[1:]).astype(jnp.int16)


def sides(odd, last):
    return (1 - odd) * last, odd * last


def odd_of(axis):
    return lax.rem(lax.axis_index(axis), 2)


def for_parity(odd, body):
    for value in (0, 1):
        pl.when(odd == value)(partial(body, value))


def send_x(part, near, far):
    def send(odd):
        x_near, x_far = sides(odd, part.shape[1] - near.shape[1])
        send_part(part, (near, 0, x_near), (far, 0, x_far))

    for_parity(odd_of("brick"), send)


def prepare_kernel(estimate, middle, near, far):
    planes, size_y = estimate.shape[:2]
    count = middle.shape[0]
    first = lax.axis_index("view") * (count - 2 * REACH) - REACH
    for y in range(0, count, 8):
        at = first + y
        inside = jnp.logical_and(at >= 0, at < size_y)
        rows = estimate[:, pl.ds(pl.multiple_of(jnp.clip(at, 0, size_y - 8), 8), 8), :]
        middle[y : y + 8] = jnp.where(inside, jnp.swapaxes(rows, 0, 1), 0.0)

    def send(odd):
        x_near, x_far = sides(odd, planes - REACH)
        near[...] = middle[:, x_near : x_near + REACH].astype(BF16)
        far[...] = middle[:, x_far : x_far + REACH].astype(BF16)

    for_parity(odd_of("brick"), send)


def deal_kernel(data, out, stage, sems):
    views, groups, core = data.shape[0], out.shape[1], out.shape[4]
    parts = [(v, q) for v in range(views) for q in range(groups)]
    loads, stores = [], []
    for n, (v, q) in enumerate(parts):
        rows = data.at[v, :, :, q * core : (q + 1) * core, :]
        loads.append(pltpu.make_async_copy(rows, stage.at[n], sems.at[0, n]))
        stores.append(pltpu.make_async_copy(stage.at[n], out.at[:, q, v], sems.at[1, n]))
    for load in loads:
        load.start()
    for load, store in zip(loads, stores):
        load.wait()
        store.start()
    for store in stores:
        store.wait()


def blur_kernel(near, middle, far, ax, ay, tz, out, fe, t1):
    views, core = ay.shape[0], ay.shape[1]

    def join(odd):
        x_near, x_far = sides(odd, REACH + core)
        fe[:, x_near : x_near + REACH] = near[...]
        fe[:, REACH : REACH + core] = middle[...].astype(BF16)
        fe[:, x_far : x_far + REACH] = far[...]

    for_parity(odd_of("brick"), join)

    def finish(v, rows):
        out[v] = rows.astype(BF16)

    blur_steps(fe, ax, ay, tz, t1, views, core, finish)


def ratio_rows(v, core, where, got, den):
    rows = [got[where[v * core + x]] for x in range(core)]
    data = jnp.concatenate(rows, axis=0).astype(F32)
    return (data / den.astype(F32)).astype(BF16)


def back_kernel(where, blurred, got, axt, ayt, tzt, out, send_near, send_far, t1):
    views, core = ayt.shape[0], got.shape[1]
    back_steps(
        lambda v: ratio_rows(v, core, where, got, blurred[v]), axt, ayt, tzt, t1, out, views, core
    )
    send_x(out, send_near, send_far)


def full_kernel(
    where, near, middle, far, total_near, total_far, got_nn, got_nf, got_fn, got_ff,
    got, ax, ay, tz, axt, ayt, tzt, kept, out, send_near, send_far, fe, t1, ratios,
):
    views, core = ay.shape[0], ay.shape[1]
    y_near, y_far = sides(odd_of("view"), out.shape[0] // 2)

    def renew(odd):
        columns = zip(
            sides(odd, core),
            sides(odd, REACH + core),
            (near, far),
            (total_near, total_far),
            ((got_nn, got_nf), (got_fn, got_ff)),
        )
        for start, x_outer, outer, total, messages in columns:
            x_inner = 2 * start + REACH - x_outer
            inner = middle.at[:, x_inner - REACH : x_inner]
            for codes, first in zip(messages, (y_near, y_far)):
                scale = scale_of(codes)

                def block(y):
                    rows, here = pl.ds(first + y, 8), pl.ds(y, 8)
                    for x, field in ((x_outer, outer), (x_inner, inner)):
                        cells = slice(x - start, x - start + REACH)
                        step = (total[rows, cells] + decode(codes[here, cells], scale)) / views
                        fresh = field[rows].astype(F32) * step
                        fe[rows, x : x + REACH] = fresh.astype(BF16)
                        if field is inner:
                            kept[rows, x - REACH : x] = fresh

                in_blocks(codes.shape[0] - 1, block)

    for_parity(odd_of("brick"), renew)

    def finish(v, rows):
        ratios[v] = ratio_rows(v, core, where, got, rows.astype(BF16))

    blur_steps(fe, ax, ay, tz, t1, views, core, finish)
    back_steps(lambda v: ratios[v], axt, ayt, tzt, t1, out, views, core)
    send_x(out, send_near, send_far)


def gather_side_kernel(which, part, got, *refs):
    out, send_near, send_far = refs[-3:]
    scale, side = scale_of(got), got.shape[1]

    def add(odd):
        x = sides(odd, side)[which]

        def block(y):
            rows = pl.ds(y, 8)
            out[rows] = part[rows, x : x + side] + decode(got[rows], scale)

        in_blocks(out.shape[0], block)

    for_parity(odd_of("brick"), add)
    y_near, y_far = sides(odd_of("view"), out.shape[0] // 2)
    send_part(out, (send_near, y_near, 0), (send_far, y_far, 0))


def gather_kernel(part, near, far, out, send_near, send_far):
    side = near.shape[1]
    off = (part.shape[1] - 2 * side) // 2
    scale_n, scale_f = scale_of(near), scale_of(far)

    def add_both(odd):
        x_near, x_far = sides(odd, side)

        def block(y):
            rows = pl.ds(y, 8)
            for got, scale, x in ((near, scale_n, x_near), (far, scale_f, x_far)):
                here = part[rows, off + x : off + x + side]
                out[rows, x : x + side] = here + decode(got[rows], scale)

        in_blocks(out.shape[0], block)

    for_parity(odd_of("brick"), add_both)
    y_near, y_far = sides(odd_of("view"), out.shape[0] - send_near.shape[0] + 1)
    send_part(out, (send_near, y_near, 0), (send_far, y_far, 0))


def last_kernel(field, total, near, far, codes_lo, codes_hi, fresh):
    y_near, y_far = sides(odd_of("view"), REACH)
    for got, first in ((near, y_near), (far, y_far)):
        scale = scale_of(got)

        def block(y):
            rows = pl.ds(REACH + first + y, 8)
            step = (total[rows] + decode(got[pl.ds(y, 8)], scale)) / VIEWS
            fresh[pl.ds(first + y, 8)] = field[rows] * step

        in_blocks(REACH, block)
    send_part(fresh, (codes_lo, 0, 0), (codes_hi, fresh.shape[0] // 2, 0))


def place_rows(message, write):
    scale = scale_of(message)
    for y in range(0, message.shape[0] - 1, 8):
        write(y, jnp.swapaxes(decode(message[y : y + 8], scale), 0, 1))


def groups_around(group, count):
    far = lax.rem(group + 2 * lax.rem(group, 2) - 1 + count, count)
    return group, group + 1 - 2 * lax.rem(group, 2), far, lax.rem(group + 2, count)


def place_kernel(groups, *refs):
    order = groups_around(lax.axis_index("view"), groups)
    out = refs[-1]
    half = refs[0].shape[0] - 1
    for n, message in enumerate(refs[:-1]):

        def write(y, rows):
            at = pl.multiple_of((2 * order[n // 2] + n % 2) * half + y, 8)
            out[:, pl.ds(at, 8), :] = rows

        place_rows(message, write)


def finish_kernel(groups, lower, upper, _, out, rows, sem):
    order = groups_around(lax.axis_index("view"), groups)
    half = lower.shape[0] - 1
    copies = []
    for n, message in enumerate((lower, upper)):

        def write(y, block):
            rows[:, n * half + y : n * half + y + 8, :] = block

        place_rows(message, write)
        at = pl.multiple_of((order[3] * 2 + n) * half, 8)
        part = rows.at[:, n * half : (n + 1) * half, :]
        copies.append(pltpu.make_async_copy(part, out.at[:, pl.ds(at, half), :], sem.at[n]))
        copies[n].start()
    for copy in copies:
        copy.wait()


VMEM = pl.BlockSpec(memory_space=pltpu.VMEM)
SMEM = pl.BlockSpec(memory_space=pltpu.SMEM)
ANY = pl.BlockSpec(memory_space=pl.ANY)


def call(kernel, out_shape, scratch, flops, *operands, scalars=0, space=VMEM, limit=36 << 20):
    size = sum(a.size * a.dtype.itemsize for a in operands)
    return pl.pallas_call(
        kernel,
        out_shape=out_shape,
        in_specs=[SMEM] * scalars + [space] * (len(operands) - scalars),
        out_specs=jax.tree.map(lambda _: space, out_shape),
        scratch_shapes=scratch,
        compiler_params=pltpu.CompilerParams(vmem_limit_bytes=limit),
        cost_estimate=pl.CostEstimate(flops=flops, bytes_accessed=size, transcendentals=0),
    )(*operands)


def halves(a, axis):
    high = lax.reduce_precision(a, 8, 7)
    return jnp.concatenate([high, a - high], axis=axis).astype(BF16)


def banded(taps, rows, cols, shift):
    offset = jnp.arange(rows)[:, None] - jnp.arange(cols)[None, :] + shift
    select = (offset[None] == jnp.arange(TAPS)[:, None, None]).astype(F32)
    return jnp.einsum("vt,trc->vrc", taps, select, precision=lax.Precision.HIGHEST)


def swap_near(a, axis):
    return lax.ppermute(a, axis, [(i, i ^ 1) for i in range(lax.axis_size(axis))])


def swap_far(a, axis, ring=False):
    count = lax.axis_size(axis)
    pairs = [(i, i + 1) for i in range(1, count - 1, 2)] + ([(count - 1, 0)] if ring else [])
    return lax.ppermute(a, axis, pairs + [(j, i) for i, j in pairs])


def per_device(estimate, view_data, psf_taps, routes):
    bricks, groups = lax.axis_size("brick"), lax.axis_size("view")
    brick, group = lax.axis_index("brick"), lax.axis_index("view")
    planes, size_y, size_z = estimate.shape
    views_dev, slots = view_data.shape[:2]
    capacity = slots // bricks
    core = size_y // groups
    ext = core + 2 * REACH
    views = views_dev * groups

    def shape(*dims, kind=F32):
        return jax.ShapeDtypeStruct(dims + (size_z,), kind)

    middle, near, far = call(
        prepare_kernel,
        (shape(ext, planes), shape(ext, REACH, kind=BF16), shape(ext, REACH, kind=BF16)),
        [],
        0,
        estimate,
    )
    near, far, psf_taps, routes = lax.optimization_barrier((near, far, psf_taps, routes))
    near, far = swap_near(near, "brick"), swap_far(far, "brick")

    normed = psf_taps / jnp.sum(psf_taps, axis=-1, keepdims=True)
    blocks = routes[..., 0].reshape(views_dev, bricks, planes)
    own = lax.dynamic_index_in_dim(blocks, brick, 1, keepdims=False)
    position = jnp.arange(planes)
    earlier = position[:, None] < position[None, :]
    rank = jnp.sum(((own[:, :, None] == own[:, None, :]) & earlier).astype(jnp.int32), axis=1)
    view_id = jnp.arange(views_dev)[:, None]
    where = ((own * groups + group) * views_dev + view_id) * capacity + rank
    packed = jnp.concatenate(
        [normed.reshape(views_dev, 3 * TAPS), where.astype(F32)], axis=1
    )
    packed = jnp.pad(packed, ((0, 0), (0, 128 - packed.shape[1])))
    across = lax.ppermute(packed, "view", [(i, (i + 2) % groups) for i in range(groups)])
    around = [packed, swap_near(packed, "view"), swap_far(packed, "view", True), across]
    order = jnp.stack([group, group ^ 1, (group + 2 * (group % 2) - 1) % groups, (group + 2) % groups])
    here = order[:, None] == jnp.arange(groups)[None, :]
    packed = jnp.sum(jnp.where(here[:, :, None, None], jnp.stack(around)[:, None], 0.0), axis=0)
    packed = packed.reshape(views, packed.shape[-1])

    sending = call(
        deal_kernel,
        shape(bricks, groups, views_dev, capacity, core, kind=BF16),
        [
            pltpu.VMEM((views_dev * groups, bricks, capacity, core, size_z), BF16),
            pltpu.SemaphoreType.DMA((2, views_dev * groups)),
        ],
        0,
        view_data.reshape(views_dev, bricks, capacity, size_y, size_z),
        space=ANY,
        limit=58 << 20,
    )
    sending = sending.reshape(bricks * groups, views_dev * capacity, core, size_z)
    sending, near, far, packed = lax.optimization_barrier((sending, near, far, packed))
    got = lax.all_to_all(sending, BOTH, 0, 0, tiled=True)
    got = got.reshape(bricks * groups * views_dev * capacity, core, size_z)

    taps = packed[:, : 3 * TAPS].reshape(views, 3, TAPS)
    where = packed[:, 3 * TAPS : 3 * TAPS + planes].astype(jnp.int32).reshape(views * planes)

    mat_x = banded(taps[:, 0], ext, planes, -1)
    mat_y = banded(taps[:, 1], ext, core, -1)
    mat_z = banded(taps[:, 2], size_z, size_z, TAPS // 2)
    ax = halves(mat_x.transpose(0, 2, 1).reshape(views * planes, ext), 1)
    ay = halves(mat_y.transpose(0, 2, 1), 2)
    tz = halves(mat_z, 1)
    axt = halves(mat_x.transpose(1, 0, 2).reshape(ext, views * planes), 0)
    ayt = halves(mat_y, 2)
    tzt = halves(mat_z.transpose(0, 2, 1), 1)

    scratch = pltpu.VMEM((views * planes, ext, size_z), F32)
    wide = pltpu.VMEM((ext, ext, size_z), BF16)
    codes = partial(shape, kind=jnp.int16)
    flops = 4 * 10**9
    rows_shape = (views, planes * core, size_z)
    forward, back = (ax, ay, tz), (axt, ayt, tzt)
    field = (near, middle, far)

    blurred = call(
        blur_kernel,
        jax.ShapeDtypeStruct(rows_shape, BF16),
        [wide, scratch],
        flops,
        *field,
        *forward,
    )
    side = 2 * REACH
    part, send_near, send_far = call(
        back_kernel,
        (shape(ext, ext),) + (codes(ext + 1, side),) * 2,
        [scratch],
        flops,
        where,
        blurred,
        got,
        *back,
        scalars=1,
    )
    side_shape = (shape(ext, side),) + (codes(side + 1, side),) * 2
    from_far, from_near = swap_far(send_far, "brick"), swap_near(send_near, "brick")
    total_near, nn, nf = call(partial(gather_side_kernel, 0), side_shape, [], 0, part, from_near)
    total_far, fn, ff = call(partial(gather_side_kernel, 1), side_shape, [], 0, part, from_far, total_near)
    side = REACH
    kept, part, send_near, send_far = call(
        full_kernel,
        (shape(ext, planes), shape(ext, ext), codes(ext + 1, side), codes(ext + 1, side)),
        [wide, scratch, pltpu.VMEM(rows_shape, BF16)],
        2 * flops,
        where,
        *field,
        total_near,
        total_far,
        swap_near(nn, "view"),
        swap_far(nf, "view"),
        swap_near(fn, "view"),
        swap_far(ff, "view"),
        got,
        *forward,
        *back,
        scalars=1,
    )
    total, send_near, send_far = call(
        gather_kernel,
        (shape(ext, planes), codes(side + 1, planes), codes(side + 1, planes)),
        [],
        0,
        part,
        swap_near(send_near, "brick"),
        swap_far(send_far, "brick"),
    )
    lower, upper = call(
        last_kernel,
        (codes(core // 2 + 1, planes),) * 2,
        [pltpu.VMEM((core, planes, size_z), F32)],
        0,
        kept,
        total,
        swap_near(send_near, "view"),
        swap_far(send_far, "view"),
    )
    lower_far, upper_near = swap_far(lower, "view", True), swap_near(upper, "view")
    upper_far, lower_near = swap_far(upper, "view", True), swap_near(lower, "view")
    lower_last, upper_last = swap_near(lower_far, "view"), swap_far(upper_near, "view", True)
    merged = call(
        partial(place_kernel, groups),
        shape(planes, size_y),
        [],
        0,
        lower,
        upper,
        lower_near,
        upper_near,
        lower_far,
        upper_far,
    )
    return pl.pallas_call(
        partial(finish_kernel, groups),
        out_shape=shape(planes, size_y),
        in_specs=[VMEM, VMEM, ANY],
        out_specs=ANY,
        scratch_shapes=[pltpu.VMEM((planes, core, size_z), F32), pltpu.SemaphoreType.DMA((2,))],
        input_output_aliases={2: 0},
        compiler_params=pltpu.CompilerParams(vmem_limit_bytes=36 << 20),
    )(lower_last, upper_last, merged)


def solution(mesh):
    return jax.shard_map(
        per_device,
        mesh=mesh,
        in_specs=(
            P("brick", None, None),
            P("view", "brick", None, None),
            P("view", None, None),
            P("view", None, None),
        ),
        out_specs=P("brick", None, None),
        check_vma=False,
    )
```

```python
from functools import partial

import jax
import jax.numpy as jnp
from jax import lax
from jax.experimental import pallas as pl
from jax.experimental.pallas import tpu as pltpu
from jax.sharding import PartitionSpec as P

VIEWS = 8
ITERS = 2
TAPS = 31
REACH = 16
BF16 = jnp.bfloat16
F32 = jnp.float32

BOTH = ("brick", "view")


def dot(a, b):
    return jnp.dot(a, b, preferred_element_type=F32)


def twice(a, axis):
    return jnp.concatenate([a, a], axis=axis)


def split(a):
    high = a.astype(BF16)
    return high, (a - high.astype(F32)).astype(BF16)


def blur_steps(fe, ax, ay, tz, t1, views, core, finish):
    ext_y = fe.shape[0]

    def along_x(step, carry):
        y0 = pl.multiple_of(step * 8, 8)
        rows = []
        for k in range(0, 8, 2):
            pair = jnp.concatenate([fe[y0 + k], fe[y0 + k + 1]], axis=1)
            out = dot(ax[...], twice(pair, 0))
            rows += [out[:, :128], out[:, 128:]]
        t1[:, pl.ds(y0, 8), :] = jnp.swapaxes(jnp.stack(rows), 0, 1)
        return carry

    lax.fori_loop(0, ext_y // 8, along_x, 0, unroll=True)

    def along_yz(v, carry):
        rows = []
        for i in range(0, core, 2):
            pair = jnp.concatenate([t1[v * core + i], t1[v * core + i + 1]], axis=1).astype(BF16)
            out = dot(ay[v], twice(pair, 0)).astype(BF16)
            rows += [out[:, :128], out[:, 128:]]
        plane = jnp.concatenate(rows, axis=0)
        finish(v, dot(twice(plane, 1), tz[v]))
        return carry

    lax.fori_loop(0, views, along_yz, 0, unroll=True)


def back_steps(ratio_of, axt, ayt, tzt, t1, out, views, core):
    def along_zy(v, carry):
        high, low = split(dot(twice(ratio_of(v), 1), tzt[v]))
        weights = twice(ayt[v], 1)
        for i in range(0, core, 2):
            here, there = slice(i * core, (i + 1) * core), slice((i + 1) * core, (i + 2) * core)
            pair = jnp.concatenate([high[here], high[there]], axis=1)
            rest = jnp.concatenate([low[here], low[there]], axis=1)
            rows = dot(weights, jnp.concatenate([pair, pair, rest, rest], axis=0))
            t1[v * core + i] = rows[:, :128]
            t1[v * core + i + 1] = rows[:, 128:]
        return carry

    lax.fori_loop(0, views, along_zy, 0, unroll=True)
    ext = out.shape[1]

    def along_x(step, carry):
        y0 = pl.multiple_of(step * 8, 8)
        high, low = split(jnp.swapaxes(t1[:, pl.ds(y0, 8), :], 0, 1))
        for k in range(0, 8, 2):
            both = dot(axt[...], jnp.concatenate([high[k], high[k + 1]], axis=1))
            rest = dot(axt[:ext], jnp.concatenate([low[k], low[k + 1]], axis=1))
            rows = both[:ext] + both[ext:] + rest
            out[y0 + k] = rows[:, :128]
            out[y0 + k + 1] = rows[:, 128:]
        return carry

    lax.fori_loop(0, out.shape[0] // 8, along_x, 0, unroll=True)


SHIFT = 256.0
LEVELS = 65534.0
HALF = 32767


def mark_of(part):
    top = jnp.max(jnp.max(part, axis=0), axis=0, keepdims=True)
    top = jnp.broadcast_to(jnp.max(top, axis=1, keepdims=True), (1, part.shape[-1]))
    return jnp.clip(jnp.ceil(jnp.log2(top)), -100.0, 120.0) + SHIFT


def encode(part, scale):
    return ((part * scale + 0.5).astype(jnp.int32) - HALF).astype(jnp.int16)


def decode(codes, scale):
    return (codes.astype(jnp.int32) + HALF).astype(F32) * scale


def scale_of(message):
    mark = message[message.shape[0] - 1, :16].astype(jnp.int32).astype(F32)[:1]
    return jnp.where(mark > 0, jnp.exp2(mark - SHIFT) / LEVELS, 0.0)


def in_blocks(count, body):
    def step(n, carry):
        body(pl.multiple_of(n * 8, 8))
        return carry

    lax.fori_loop(0, count // 8, step, 0, unroll=True)


def send_part(part, *messages):
    mark = mark_of(part[...])
    scale = jnp.exp2(SHIFT - mark) * LEVELS
    for out, y0, x0 in messages:
        count, width = out.shape[0] - 1, out.shape[1]

        def block(y):
            out[pl.ds(y, 8)] = encode(part[pl.ds(y0 + y, 8), x0 : x0 + width], scale)

        in_blocks(count, block)
        out[count] = jnp.broadcast_to(mark.astype(jnp.int32), out.shape[1:]).astype(jnp.int16)


def sides(odd, last):
    return (1 - odd) * last, odd * last


def odd_of(axis):
    return lax.rem(lax.axis_index(axis), 2)


def for_parity(odd, body):
    for value in (0, 1):
        pl.when(odd == value)(partial(body, value))


def send_x(part, near, far):
    def send(odd):
        x_near, x_far = sides(odd, part.shape[1] - near.shape[1])
        send_part(part, (near, 0, x_near), (far, 0, x_far))

    for_parity(odd_of("brick"), send)


def prepare_kernel(estimate, middle, near, far):
    planes, size_y = estimate.shape[:2]
    count = middle.shape[0]
    first = lax.axis_index("view") * (count - 2 * REACH) - REACH
    for y in range(0, count, 8):
        at = first + y
        inside = jnp.logical_and(at >= 0, at < size_y)
        rows = estimate[:, pl.ds(pl.multiple_of(jnp.clip(at, 0, size_y - 8), 8), 8), :]
        middle[y : y + 8] = jnp.where(inside, jnp.swapaxes(rows, 0, 1), 0.0)

    def send(odd):
        x_near, x_far = sides(odd, planes - REACH)
        near[...] = middle[:, x_near : x_near + REACH].astype(BF16)
        far[...] = middle[:, x_far : x_far + REACH].astype(BF16)

    for_parity(odd_of("brick"), send)


def deal_kernel(data, out, stage, sems):
    views, groups, core = data.shape[0], out.shape[1], out.shape[4]
    parts = [(v, q) for v in range(views) for q in range(groups)]
    loads, stores = [], []
    for n, (v, q) in enumerate(parts):
        rows = data.at[v, :, :, q * core : (q + 1) * core, :]
        loads.append(pltpu.make_async_copy(rows, stage.at[n], sems.at[0, n]))
        stores.append(pltpu.make_async_copy(stage.at[n], out.at[:, q, v], sems.at[1, n]))
    for load in loads:
        load.start()
    for load, store in zip(loads, stores):
        load.wait()
        store.start()
    for store in stores:
        store.wait()


def blur_kernel(near, middle, far, ax, ay, tz, out, fe, t1):
    views, core = ay.shape[0], ay.shape[1]

    def join(odd):
        x_near, x_far = sides(odd, REACH + core)
        fe[:, x_near : x_near + REACH] = near[...]
        fe[:, REACH : REACH + core] = middle[...].astype(BF16)
        fe[:, x_far : x_far + REACH] = far[...]

    for_parity(odd_of("brick"), join)

    def finish(v, rows):
        out[v] = rows.astype(BF16)

    blur_steps(fe, ax, ay, tz, t1, views, core, finish)


def ratio_rows(v, core, where, got, den):
    rows = [got[where[v * core + x]] for x in range(core)]
    data = jnp.concatenate(rows, axis=0).astype(F32)
    return (data / den.astype(F32)).astype(BF16)


def back_kernel(where, blurred, got, axt, ayt, tzt, out, send_near, send_far, t1):
    views, core = ayt.shape[0], got.shape[1]
    back_steps(
        lambda v: ratio_rows(v, core, where, got, blurred[v]), axt, ayt, tzt, t1, out, views, core
    )
    send_x(out, send_near, send_far)


def full_kernel(
    where, near, middle, far, total_near, total_far, got_nn, got_nf, got_fn, got_ff,
    got, ax, ay, tz, axt, ayt, tzt, kept, out, send_near, send_far, fe, t1, ratios,
):
    views, core = ay.shape[0], ay.shape[1]
    y_near, y_far = sides(odd_of("view"), out.shape[0] // 2)

    def renew(odd):
        columns = zip(
            sides(odd, core),
            sides(odd, REACH + core),
            (near, far),
            (total_near, total_far),
            ((got_nn, got_nf), (got_fn, got_ff)),
        )
        for start, x_outer, outer, total, messages in columns:
            x_inner = 2 * start + REACH - x_outer
            inner = middle.at[:, x_inner - REACH : x_inner]
            for codes, first in zip(messages, (y_near, y_far)):
                scale = scale_of(codes)

                def block(y):
                    rows, here = pl.ds(first + y, 8), pl.ds(y, 8)
                    for x, field in ((x_outer, outer), (x_inner, inner)):
                        cells = slice(x - start, x - start + REACH)
                        step = (total[rows, cells] + decode(codes[here, cells], scale)) / views
                        fresh = field[rows].astype(F32) * step
                        fe[rows, x : x + REACH] = fresh.astype(BF16)
                        if field is inner:
                            kept[rows, x - REACH : x] = fresh

                in_blocks(codes.shape[0] - 1, block)

    for_parity(odd_of("brick"), renew)

    def finish(v, rows):
        ratios[v] = ratio_rows(v, core, where, got, rows.astype(BF16))

    blur_steps(fe, ax, ay, tz, t1, views, core, finish)
    back_steps(lambda v: ratios[v], axt, ayt, tzt, t1, out, views, core)
    send_x(out, send_near, send_far)


def gather_side_kernel(which, part, got, *refs):
    out, send_near, send_far = refs[-3:]
    scale, side = scale_of(got), got.shape[1]

    def add(odd):
        x = sides(odd, side)[which]

        def block(y):
            rows = pl.ds(y, 8)
            out[rows] = part[rows, x : x + side] + decode(got[rows], scale)

        in_blocks(out.shape[0], block)

    for_parity(odd_of("brick"), add)
    y_near, y_far = sides(odd_of("view"), out.shape[0] // 2)
    send_part(out, (send_near, y_near, 0), (send_far, y_far, 0))


def gather_kernel(part, near, far, out, send_near, send_far):
    side = near.shape[1]
    off = (part.shape[1] - 2 * side) // 2
    scale_n, scale_f = scale_of(near), scale_of(far)

    def add_both(odd):
        x_near, x_far = sides(odd, side)

        def block(y):
            rows = pl.ds(y, 8)
            for got, scale, x in ((near, scale_n, x_near), (far, scale_f, x_far)):
                here = part[rows, off + x : off + x + side]
                out[rows, x : x + side] = here + decode(got[rows], scale)

        in_blocks(out.shape[0], block)

    for_parity(odd_of("brick"), add_both)
    y_near, y_far = sides(odd_of("view"), out.shape[0] - send_near.shape[0] + 1)
    send_part(out, (send_near, y_near, 0), (send_far, y_far, 0))


def last_kernel(field, total, near, far, codes_lo, codes_hi, fresh):
    y_near, y_far = sides(odd_of("view"), REACH)
    for got, first in ((near, y_near), (far, y_far)):
        scale = scale_of(got)

        def block(y):
            rows = pl.ds(REACH + first + y, 8)
            step = (total[rows] + decode(got[pl.ds(y, 8)], scale)) / VIEWS
            fresh[pl.ds(first + y, 8)] = field[rows] * step

        in_blocks(REACH, block)
    send_part(fresh, (codes_lo, 0, 0), (codes_hi, fresh.shape[0] // 2, 0))


def place_rows(message, write):
    scale = scale_of(message)
    for y in range(0, message.shape[0] - 1, 8):
        write(y, jnp.swapaxes(decode(message[y : y + 8], scale), 0, 1))


def groups_around(group, count):
    far = lax.rem(group + 2 * lax.rem(group, 2) - 1 + count, count)
    return group, group + 1 - 2 * lax.rem(group, 2), far, lax.rem(group + 2, count)


def place_kernel(groups, *refs):
    order = groups_around(lax.axis_index("view"), groups)
    out = refs[-1]
    half = refs[0].shape[0] - 1
    for n, message in enumerate(refs[:-1]):

        def write(y, rows):
            at = pl.multiple_of((2 * order[n // 2] + n % 2) * half + y, 8)
            out[:, pl.ds(at, 8), :] = rows

        place_rows(message, write)


def finish_kernel(groups, lower, upper, _, out, rows, sem):
    order = groups_around(lax.axis_index("view"), groups)
    half = lower.shape[0] - 1
    copies = []
    for n, message in enumerate((lower, upper)):

        def write(y, block):
            rows[:, n * half + y : n * half + y + 8, :] = block

        place_rows(message, write)
        at = pl.multiple_of((order[3] * 2 + n) * half, 8)
        part = rows.at[:, n * half : (n + 1) * half, :]
        copies.append(pltpu.make_async_copy(part, out.at[:, pl.ds(at, half), :], sem.at[n]))
        copies[n].start()
    for copy in copies:
        copy.wait()


VMEM = pl.BlockSpec(memory_space=pltpu.VMEM)
SMEM = pl.BlockSpec(memory_space=pltpu.SMEM)
ANY = pl.BlockSpec(memory_space=pl.ANY)


def call(kernel, out_shape, scratch, flops, *operands, scalars=0, space=VMEM, limit=36 << 20):
    size = sum(a.size * a.dtype.itemsize for a in operands)
    return pl.pallas_call(
        kernel,
        out_shape=out_shape,
        in_specs=[SMEM] * scalars + [space] * (len(operands) - scalars),
        out_specs=jax.tree.map(lambda _: space, out_shape),
        scratch_shapes=scratch,
        compiler_params=pltpu.CompilerParams(vmem_limit_bytes=limit),
        cost_estimate=pl.CostEstimate(flops=flops, bytes_accessed=size, transcendentals=0),
    )(*operands)


def halves(a, axis):
    high = lax.reduce_precision(a, 8, 7)
    return jnp.concatenate([high, a - high], axis=axis).astype(BF16)


def banded(taps, rows, cols, shift):
    offset = jnp.arange(rows)[:, None] - jnp.arange(cols)[None, :] + shift
    select = (offset[None] == jnp.arange(TAPS)[:, None, None]).astype(F32)
    return jnp.einsum("vt,trc->vrc", taps, select, precision=lax.Precision.HIGHEST)


def swap_near(a, axis):
    return lax.ppermute(a, axis, [(i, i ^ 1) for i in range(lax.axis_size(axis))])


def swap_far(a, axis, ring=False):
    count = lax.axis_size(axis)
    pairs = [(i, i + 1) for i in range(1, count - 1, 2)] + ([(count - 1, 0)] if ring else [])
    return lax.ppermute(a, axis, pairs + [(j, i) for i, j in pairs])


def per_device(estimate, view_data, psf_taps, routes):
    bricks, groups = lax.axis_size("brick"), lax.axis_size("view")
    brick, group = lax.axis_index("brick"), lax.axis_index("view")
    planes, size_y, size_z = estimate.shape
    views_dev, slots = view_data.shape[:2]
    capacity = slots // bricks
    core = size_y // groups
    ext = core + 2 * REACH
    views = views_dev * groups

    def shape(*dims, kind=F32):
        return jax.ShapeDtypeStruct(dims + (size_z,), kind)

    middle, near, far = call(
        prepare_kernel,
        (shape(ext, planes), shape(ext, REACH, kind=BF16), shape(ext, REACH, kind=BF16)),
        [],
        0,
        estimate,
    )
    near, far, psf_taps, routes = lax.optimization_barrier((near, far, psf_taps, routes))
    near, far = swap_near(near, "brick"), swap_far(far, "brick")

    normed = psf_taps / jnp.sum(psf_taps, axis=-1, keepdims=True)
    blocks = routes[..., 0].reshape(views_dev, bricks, planes)
    own = lax.dynamic_index_in_dim(blocks, brick, 1, keepdims=False)
    position = jnp.arange(planes)
    earlier = position[:, None] < position[None, :]
    rank = jnp.sum(((own[:, :, None] == own[:, None, :]) & earlier).astype(jnp.int32), axis=1)
    view_id = jnp.arange(views_dev)[:, None]
    where = ((own * groups + group) * views_dev + view_id) * capacity + rank
    packed = jnp.concatenate(
        [normed.reshape(views_dev, 3 * TAPS), where.astype(F32)], axis=1
    )
    packed = jnp.pad(packed, ((0, 0), (0, 128 - packed.shape[1])))
    across = lax.ppermute(packed, "view", [(i, (i + 2) % groups) for i in range(groups)])
    around = [packed, swap_near(packed, "view"), swap_far(packed, "view", True), across]
    order = jnp.stack([group, group ^ 1, (group + 2 * (group % 2) - 1) % groups, (group + 2) % groups])
    here = order[:, None] == jnp.arange(groups)[None, :]
    packed = jnp.sum(jnp.where(here[:, :, None, None], jnp.stack(around)[:, None], 0.0), axis=0)
    packed = packed.reshape(views, packed.shape[-1])

    sending = call(
        deal_kernel,
        shape(bricks, groups, views_dev, capacity, core, kind=BF16),
        [
            pltpu.VMEM((views_dev * groups, bricks, capacity, core, size_z), BF16),
            pltpu.SemaphoreType.DMA((2, views_dev * groups)),
        ],
        0,
        view_data.reshape(views_dev, bricks, capacity, size_y, size_z),
        space=ANY,
        limit=58 << 20,
    )
    sending = sending.reshape(bricks * groups, views_dev * capacity, core, size_z)
    sending, near, far, packed = lax.optimization_barrier((sending, near, far, packed))
    got = lax.all_to_all(sending, BOTH, 0, 0, tiled=True)
    got = got.reshape(bricks * groups * views_dev * capacity, core, size_z)

    taps = packed[:, : 3 * TAPS].reshape(views, 3, TAPS)
    where = packed[:, 3 * TAPS : 3 * TAPS + planes].astype(jnp.int32).reshape(views * planes)

    mat_x = banded(taps[:, 0], ext, planes, -1)
    mat_y = banded(taps[:, 1], ext, core, -1)
    mat_z = banded(taps[:, 2], size_z, size_z, TAPS // 2)
    ax = halves(mat_x.transpose(0, 2, 1).reshape(views * planes, ext), 1)
    ay = halves(mat_y.transpose(0, 2, 1), 2)
    tz = halves(mat_z, 1)
    axt = halves(mat_x.transpose(1, 0, 2).reshape(ext, views * planes), 0)
    ayt = halves(mat_y, 2)
    tzt = halves(mat_z.transpose(0, 2, 1), 1)

    scratch = pltpu.VMEM((views * planes, ext, size_z), F32)
    wide = pltpu.VMEM((ext, ext, size_z), BF16)
    codes = partial(shape, kind=jnp.int16)
    flops = 4 * 10**9
    rows_shape = (views, planes * core, size_z)
    forward, back = (ax, ay, tz), (axt, ayt, tzt)
    field = (near, middle, far)

    blurred = call(
        blur_kernel,
        jax.ShapeDtypeStruct(rows_shape, BF16),
        [wide, scratch],
        flops,
        *field,
        *forward,
    )
    side = 2 * REACH
    part, send_near, send_far = call(
        back_kernel,
        (shape(ext, ext),) + (codes(ext + 1, side),) * 2,
        [scratch],
        flops,
        where,
        blurred,
        got,
        *back,
        scalars=1,
    )
    side_shape = (shape(ext, side),) + (codes(side + 1, side),) * 2
    from_far, from_near = swap_far(send_far, "brick"), swap_near(send_near, "brick")
    total_near, nn, nf = call(partial(gather_side_kernel, 0), side_shape, [], 0, part, from_near)
    total_far, fn, ff = call(partial(gather_side_kernel, 1), side_shape, [], 0, part, from_far, total_near)
    side = REACH
    kept, part, send_near, send_far = call(
        full_kernel,
        (shape(ext, planes), shape(ext, ext), codes(ext + 1, side), codes(ext + 1, side)),
        [wide, scratch, pltpu.VMEM(rows_shape, BF16)],
        2 * flops,
        where,
        *field,
        total_near,
        total_far,
        swap_near(nn, "view"),
        swap_far(nf, "view"),
        swap_near(fn, "view"),
        swap_far(ff, "view"),
        got,
        *forward,
        *back,
        scalars=1,
    )
    total, send_near, send_far = call(
        gather_kernel,
        (shape(ext, planes), codes(side + 1, planes), codes(side + 1, planes)),
        [],
        0,
        part,
        swap_near(send_near, "brick"),
        swap_far(send_far, "brick"),
    )
    lower, upper = call(
        last_kernel,
        (codes(core // 2 + 1, planes),) * 2,
        [pltpu.VMEM((core, planes, size_z), F32)],
        0,
        kept,
        total,
        swap_near(send_near, "view"),
        swap_far(send_far, "view"),
    )
    lower_far, upper_near = swap_far(lower, "view", True), swap_near(upper, "view")
    upper_far, lower_near = swap_far(upper, "view", True), swap_near(lower, "view")
    lower_last, upper_last = swap_near(lower_far, "view"), swap_far(upper_near, "view", True)
    merged = call(
        partial(place_kernel, groups),
        shape(planes, size_y),
        [],
        0,
        lower,
        upper,
        lower_near,
        upper_near,
        lower_far,
        upper_far,
    )
    return pl.pallas_call(
        partial(finish_kernel, groups),
        out_shape=shape(planes, size_y),
        in_specs=[VMEM, VMEM, ANY],
        out_specs=ANY,
        scratch_shapes=[pltpu.VMEM((planes, core, size_z), F32), pltpu.SemaphoreType.DMA((2,))],
        input_output_aliases={2: 0},
        compiler_params=pltpu.CompilerParams(vmem_limit_bytes=36 << 20),
    )(lower_last, upper_last, merged)


def solution(mesh):
    return jax.shard_map(
        per_device,
        mesh=mesh,
        in_specs=(
            P("brick", None, None),
            P("view", "brick", None, None),
            P("view", None, None),
            P("view", None, None),
        ),
        out_specs=P("brick", None, None),
        check_vma=False,
    )
```

```python
from functools import partial

import jax
import jax.numpy as jnp
from jax import lax
from jax.experimental import pallas as pl
from jax.experimental.pallas import tpu as pltpu
from jax.sharding import PartitionSpec as P

VIEWS = 8
ITERS = 2
TAPS = 31
REACH = 16
BF16 = jnp.bfloat16
F32 = jnp.float32

BOTH = ("brick", "view")


def dot(a, b):
    return jnp.dot(a, b, preferred_element_type=F32)


def twice(a, axis):
    return jnp.concatenate([a, a], axis=axis)


def split(a):
    high = a.astype(BF16)
    return high, (a - high.astype(F32)).astype(BF16)


def blur_steps(fe, ax, ay, tz, t1, views, core, finish):
    ext_y = fe.shape[0]

    def along_x(step, carry):
        y0 = pl.multiple_of(step * 8, 8)
        rows = []
        for k in range(0, 8, 2):
            pair = jnp.concatenate([fe[y0 + k], fe[y0 + k + 1]], axis=1)
            out = dot(ax[...], twice(pair, 0))
            rows += [out[:, :128], out[:, 128:]]
        t1[:, pl.ds(y0, 8), :] = jnp.swapaxes(jnp.stack(rows), 0, 1)
        return carry

    lax.fori_loop(0, ext_y // 8, along_x, 0, unroll=True)

    def along_yz(v, carry):
        rows = []
        for i in range(0, core, 2):
            pair = jnp.concatenate([t1[v * core + i], t1[v * core + i + 1]], axis=1).astype(BF16)
            out = dot(ay[v], twice(pair, 0)).astype(BF16)
            rows += [out[:, :128], out[:, 128:]]
        plane = jnp.concatenate(rows, axis=0)
        finish(v, dot(twice(plane, 1), tz[v]))
        return carry

    lax.fori_loop(0, views, along_yz, 0, unroll=True)


def back_steps(ratio_of, axt, ayt, tzt, t1, out, views, core):
    def along_zy(v, carry):
        high, low = split(dot(twice(ratio_of(v), 1), tzt[v]))
        weights = twice(ayt[v], 1)
        for i in range(0, core, 2):
            here, there = slice(i * core, (i + 1) * core), slice((i + 1) * core, (i + 2) * core)
            pair = jnp.concatenate([high[here], high[there]], axis=1)
            rest = jnp.concatenate([low[here], low[there]], axis=1)
            rows = dot(weights, jnp.concatenate([pair, pair, rest, rest], axis=0))
            t1[v * core + i] = rows[:, :128]
            t1[v * core + i + 1] = rows[:, 128:]
        return carry

    lax.fori_loop(0, views, along_zy, 0, unroll=True)
    ext = out.shape[1]

    def along_x(step, carry):
        y0 = pl.multiple_of(step * 8, 8)
        high, low = split(jnp.swapaxes(t1[:, pl.ds(y0, 8), :], 0, 1))
        for k in range(0, 8, 2):
            both = dot(axt[...], jnp.concatenate([high[k], high[k + 1]], axis=1))
            rest = dot(axt[:ext], jnp.concatenate([low[k], low[k + 1]], axis=1))
            rows = both[:ext] + both[ext:] + rest
            out[y0 + k] = rows[:, :128]
            out[y0 + k + 1] = rows[:, 128:]
        return carry

    lax.fori_loop(0, out.shape[0] // 8, along_x, 0, unroll=True)


SHIFT = 256.0
LEVELS = 65534.0
HALF = 32767


def mark_of(part):
    top = jnp.max(jnp.max(part, axis=0), axis=0, keepdims=True)
    top = jnp.broadcast_to(jnp.max(top, axis=1, keepdims=True), (1, part.shape[-1]))
    return jnp.clip(jnp.ceil(jnp.log2(top)), -100.0, 120.0) + SHIFT


def encode(part, scale):
    return ((part * scale + 0.5).astype(jnp.int32) - HALF).astype(jnp.int16)


def decode(codes, scale):
    return (codes.astype(jnp.int32) + HALF).astype(F32) * scale


def scale_of(message):
    mark = message[message.shape[0] - 1, :16].astype(jnp.int32).astype(F32)[:1]
    return jnp.where(mark > 0, jnp.exp2(mark - SHIFT) / LEVELS, 0.0)


def in_blocks(count, body):
    def step(n, carry):
        body(pl.multiple_of(n * 8, 8))
        return carry

    lax.fori_loop(0, count // 8, step, 0)


def send_part(part, *messages):
    mark = mark_of(part[...])
    scale = jnp.exp2(SHIFT - mark) * LEVELS
    for out, y0, x0 in messages:
        count, width = out.shape[0] - 1, out.shape[1]

        def block(y):
            out[pl.ds(y, 8)] = encode(part[pl.ds(y0 + y, 8), x0 : x0 + width], scale)

        in_blocks(count, block)
        out[count] = jnp.broadcast_to(mark.astype(jnp.int32), out.shape[1:]).astype(jnp.int16)


def sides(odd, last):
    return (1 - odd) * last, odd * last


def odd_of(axis):
    return lax.rem(lax.axis_index(axis), 2)


def for_parity(odd, body):
    for value in (0, 1):
        pl.when(odd == value)(partial(body, value))


def send_x(part, near, far):
    def send(odd):
        x_near, x_far = sides(odd, part.shape[1] - near.shape[1])
        send_part(part, (near, 0, x_near), (far, 0, x_far))

    for_parity(odd_of("brick"), send)


def prepare_kernel(estimate, middle, near, far):
    planes, size_y = estimate.shape[:2]
    count = middle.shape[0]
    first = lax.axis_index("view") * (count - 2 * REACH) - REACH
    for y in range(0, count, 8):
        at = first + y
        inside = jnp.logical_and(at >= 0, at < size_y)
        rows = estimate[:, pl.ds(pl.multiple_of(jnp.clip(at, 0, size_y - 8), 8), 8), :]
        middle[y : y + 8] = jnp.where(inside, jnp.swapaxes(rows, 0, 1), 0.0)

    def send(odd):
        x_near, x_far = sides(odd, planes - REACH)
        near[...] = middle[:, x_near : x_near + REACH].astype(BF16)
        far[...] = middle[:, x_far : x_far + REACH].astype(BF16)

    for_parity(odd_of("brick"), send)


def deal_kernel(data, out, stage, sems):
    views, groups, core = data.shape[0], out.shape[1], out.shape[4]
    parts = [(v, q) for v in range(views) for q in range(groups)]
    loads, stores = [], []
    for n, (v, q) in enumerate(parts):
        rows = data.at[v, :, :, q * core : (q + 1) * core, :]
        loads.append(pltpu.make_async_copy(rows, stage.at[n], sems.at[0, n]))
        stores.append(pltpu.make_async_copy(stage.at[n], out.at[:, q, v], sems.at[1, n]))
    for load in loads:
        load.start()
    for load, store in zip(loads, stores):
        load.wait()
        store.start()
    for store in stores:
        store.wait()


def blur_kernel(near, middle, far, ax, ay, tz, out, fe, t1):
    views, core = ay.shape[0], ay.shape[1]

    def join(odd):
        x_near, x_far = sides(odd, REACH + core)
        fe[:, x_near : x_near + REACH] = near[...]
        fe[:, REACH : REACH + core] = middle[...].astype(BF16)
        fe[:, x_far : x_far + REACH] = far[...]

    for_parity(odd_of("brick"), join)

    def finish(v, rows):
        out[v] = rows.astype(BF16)

    blur_steps(fe, ax, ay, tz, t1, views, core, finish)


def ratio_rows(v, core, where, got, den):
    rows = [got[where[v * core + x]] for x in range(core)]
    data = jnp.concatenate(rows, axis=0).astype(F32)
    return (data / den.astype(F32)).astype(BF16)


def back_kernel(where, blurred, got, axt, ayt, tzt, out, send_near, send_far, t1):
    views, core = ayt.shape[0], got.shape[1]
    back_steps(
        lambda v: ratio_rows(v, core, where, got, blurred[v]), axt, ayt, tzt, t1, out, views, core
    )
    send_x(out, send_near, send_far)


def full_kernel(
    where, near, middle, far, total_near, total_far, got_nn, got_nf, got_fn, got_ff,
    got, ax, ay, tz, axt, ayt, tzt, kept, out, send_near, send_far, fe, t1, ratios,
):
    views, core = ay.shape[0], ay.shape[1]
    y_near, y_far = sides(odd_of("view"), out.shape[0] // 2)

    def renew(odd):
        columns = zip(
            sides(odd, core),
            sides(odd, REACH + core),
            (near, far),
            (total_near, total_far),
            ((got_nn, got_nf), (got_fn, got_ff)),
        )
        for start, x_outer, outer, total, messages in columns:
            x_inner = 2 * start + REACH - x_outer
            inner = middle.at[:, x_inner - REACH : x_inner]
            for codes, first in zip(messages, (y_near, y_far)):
                scale = scale_of(codes)

                def block(y):
                    rows, here = pl.ds(first + y, 8), pl.ds(y, 8)
                    for x, field in ((x_outer, outer), (x_inner, inner)):
                        cells = slice(x - start, x - start + REACH)
                        step = (total[rows, cells] + decode(codes[here, cells], scale)) / views
                        fresh = field[rows].astype(F32) * step
                        fe[rows, x : x + REACH] = fresh.astype(BF16)
                        if field is inner:
                            kept[rows, x - REACH : x] = fresh

                in_blocks(codes.shape[0] - 1, block)

    for_parity(odd_of("brick"), renew)

    def finish(v, rows):
        ratios[v] = ratio_rows(v, core, where, got, rows.astype(BF16))

    blur_steps(fe, ax, ay, tz, t1, views, core, finish)
    back_steps(lambda v: ratios[v], axt, ayt, tzt, t1, out, views, core)
    send_x(out, send_near, send_far)


def gather_side_kernel(which, part, got, *refs):
    out, send_near, send_far = refs[-3:]
    scale, side = scale_of(got), got.shape[1]

    def add(odd):
        x = sides(odd, side)[which]

        def block(y):
            rows = pl.ds(y, 8)
            out[rows] = part[rows, x : x + side] + decode(got[rows], scale)

        in_blocks(out.shape[0], block)

    for_parity(odd_of("brick"), add)
    y_near, y_far = sides(odd_of("view"), out.shape[0] // 2)
    send_part(out, (send_near, y_near, 0), (send_far, y_far, 0))


def gather_kernel(part, near, far, out, send_near, send_far):
    side = near.shape[1]
    off = (part.shape[1] - 2 * side) // 2
    scale_n, scale_f = scale_of(near), scale_of(far)

    def add_both(odd):
        x_near, x_far = sides(odd, side)

        def block(y):
            rows = pl.ds(y, 8)
            for got, scale, x in ((near, scale_n, x_near), (far, scale_f, x_far)):
                here = part[rows, off + x : off + x + side]
                out[rows, x : x + side] = here + decode(got[rows], scale)

        in_blocks(out.shape[0], block)

    for_parity(odd_of("brick"), add_both)
    y_near, y_far = sides(odd_of("view"), out.shape[0] - send_near.shape[0] + 1)
    send_part(out, (send_near, y_near, 0), (send_far, y_far, 0))


def last_kernel(field, total, near, far, codes_lo, codes_hi, fresh):
    y_near, y_far = sides(odd_of("view"), REACH)
    for got, first in ((near, y_near), (far, y_far)):
        scale = scale_of(got)

        def block(y):
            rows = pl.ds(REACH + first + y, 8)
            step = (total[rows] + decode(got[pl.ds(y, 8)], scale)) / VIEWS
            fresh[pl.ds(first + y, 8)] = field[rows] * step

        in_blocks(REACH, block)
    send_part(fresh, (codes_lo, 0, 0), (codes_hi, fresh.shape[0] // 2, 0))


def place_rows(message, write):
    scale = scale_of(message)
    for y in range(0, message.shape[0] - 1, 8):
        write(y, jnp.swapaxes(decode(message[y : y + 8], scale), 0, 1))


def groups_around(group, count):
    far = lax.rem(group + 2 * lax.rem(group, 2) - 1 + count, count)
    return group, group + 1 - 2 * lax.rem(group, 2), far, lax.rem(group + 2, count)


def place_kernel(groups, *refs):
    order = groups_around(lax.axis_index("view"), groups)
    out = refs[-1]
    half = refs[0].shape[0] - 1
    for n, message in enumerate(refs[:-1]):

        def write(y, rows):
            at = pl.multiple_of((2 * order[n // 2] + n % 2) * half + y, 8)
            out[:, pl.ds(at, 8), :] = rows

        place_rows(message, write)


def finish_kernel(groups, lower, upper, _, out, rows, sem):
    order = groups_around(lax.axis_index("view"), groups)
    half = lower.shape[0] - 1
    copies = []
    for n, message in enumerate((lower, upper)):

        def write(y, block):
            rows[:, n * half + y : n * half + y + 8, :] = block

        place_rows(message, write)
        at = pl.multiple_of((order[3] * 2 + n) * half, 8)
        part = rows.at[:, n * half : (n + 1) * half, :]
        copies.append(pltpu.make_async_copy(part, out.at[:, pl.ds(at, half), :], sem.at[n]))
        copies[n].start()
    for copy in copies:
        copy.wait()


VMEM = pl.BlockSpec(memory_space=pltpu.VMEM)
SMEM = pl.BlockSpec(memory_space=pltpu.SMEM)
ANY = pl.BlockSpec(memory_space=pl.ANY)


def call(kernel, out_shape, scratch, flops, *operands, scalars=0, space=VMEM, limit=36 << 20):
    size = sum(a.size * a.dtype.itemsize for a in operands)
    return pl.pallas_call(
        kernel,
        out_shape=out_shape,
        in_specs=[SMEM] * scalars + [space] * (len(operands) - scalars),
        out_specs=jax.tree.map(lambda _: space, out_shape),
        scratch_shapes=scratch,
        compiler_params=pltpu.CompilerParams(vmem_limit_bytes=limit),
        cost_estimate=pl.CostEstimate(flops=flops, bytes_accessed=size, transcendentals=0),
    )(*operands)


def halves(a, axis):
    high = lax.reduce_precision(a, 8, 7)
    return jnp.concatenate([high, a - high], axis=axis).astype(BF16)


def banded(taps, rows, cols, shift):
    offset = jnp.arange(rows)[:, None] - jnp.arange(cols)[None, :] + shift
    select = (offset[None] == jnp.arange(TAPS)[:, None, None]).astype(F32)
    return jnp.einsum("vt,trc->vrc", taps, select, precision=lax.Precision.HIGHEST)


def swap_near(a, axis):
    return lax.ppermute(a, axis, [(i, i ^ 1) for i in range(lax.axis_size(axis))])


def swap_far(a, axis, ring=False):
    count = lax.axis_size(axis)
    pairs = [(i, i + 1) for i in range(1, count - 1, 2)] + ([(count - 1, 0)] if ring else [])
    return lax.ppermute(a, axis, pairs + [(j, i) for i, j in pairs])


def per_device(estimate, view_data, psf_taps, routes):
    bricks, groups = lax.axis_size("brick"), lax.axis_size("view")
    brick, group = lax.axis_index("brick"), lax.axis_index("view")
    planes, size_y, size_z = estimate.shape
    views_dev, slots = view_data.shape[:2]
    capacity = slots // bricks
    core = size_y // groups
    ext = core + 2 * REACH
    views = views_dev * groups

    def shape(*dims, kind=F32):
        return jax.ShapeDtypeStruct(dims + (size_z,), kind)

    middle, near, far = call(
        prepare_kernel,
        (shape(ext, planes), shape(ext, REACH, kind=BF16), shape(ext, REACH, kind=BF16)),
        [],
        0,
        estimate,
    )
    near, far, psf_taps, routes = lax.optimization_barrier((near, far, psf_taps, routes))
    near, far = swap_near(near, "brick"), swap_far(far, "brick")

    normed = psf_taps / jnp.sum(psf_taps, axis=-1, keepdims=True)
    blocks = routes[..., 0].reshape(views_dev, bricks, planes)
    own = lax.dynamic_index_in_dim(blocks, brick, 1, keepdims=False)
    position = jnp.arange(planes)
    earlier = position[:, None] < position[None, :]
    rank = jnp.sum(((own[:, :, None] == own[:, None, :]) & earlier).astype(jnp.int32), axis=1)
    view_id = jnp.arange(views_dev)[:, None]
    where = ((own * groups + group) * views_dev + view_id) * capacity + rank
    packed = jnp.concatenate(
        [normed.reshape(views_dev, 3 * TAPS), where.astype(F32)], axis=1
    )
    packed = jnp.pad(packed, ((0, 0), (0, 128 - packed.shape[1])))
    mine = jnp.concatenate([packed, swap_near(packed, "view")])
    around = jnp.split(jnp.concatenate([mine, swap_far(mine, "view", True)]), groups)
    order = jnp.stack([group, group ^ 1, (group + 2 * (group % 2) - 1) % groups, (group + 2) % groups])
    here = order[:, None] == jnp.arange(groups)[None, :]
    packed = jnp.sum(jnp.where(here[:, :, None, None], jnp.stack(around)[:, None], 0.0), axis=0)
    packed = packed.reshape(views, packed.shape[-1])

    sending = call(
        deal_kernel,
        shape(bricks, groups, views_dev, capacity, core, kind=BF16),
        [
            pltpu.VMEM((views_dev * groups, bricks, capacity, core, size_z), BF16),
            pltpu.SemaphoreType.DMA((2, views_dev * groups)),
        ],
        0,
        view_data.reshape(views_dev, bricks, capacity, size_y, size_z),
        space=ANY,
        limit=58 << 20,
    )
    sending = sending.reshape(bricks * groups, views_dev * capacity, core, size_z)
    sending, near, far, packed = lax.optimization_barrier((sending, near, far, packed))
    got = lax.all_to_all(sending, BOTH, 0, 0, tiled=True)
    got = got.reshape(bricks * groups * views_dev * capacity, core, size_z)

    taps = packed[:, : 3 * TAPS].reshape(views, 3, TAPS)
    where = packed[:, 3 * TAPS : 3 * TAPS + planes].astype(jnp.int32).reshape(views * planes)

    mat_x = banded(taps[:, 0], ext, planes, -1)
    mat_y = banded(taps[:, 1], ext, core, -1)
    mat_z = banded(taps[:, 2], size_z, size_z, TAPS // 2)
    ax = halves(mat_x.transpose(0, 2, 1).reshape(views * planes, ext), 1)
    ay = halves(mat_y.transpose(0, 2, 1), 2)
    tz = halves(mat_z, 1)
    axt = halves(mat_x.transpose(1, 0, 2).reshape(ext, views * planes), 0)
    ayt = halves(mat_y, 2)
    tzt = halves(mat_z.transpose(0, 2, 1), 1)

    scratch = pltpu.VMEM((views * planes, ext, size_z), F32)
    wide = pltpu.VMEM((ext, ext, size_z), BF16)
    codes = partial(shape, kind=jnp.int16)
    flops = 4 * 10**9
    rows_shape = (views, planes * core, size_z)
    forward, back = (ax, ay, tz), (axt, ayt, tzt)
    field = (near, middle, far)

    blurred = call(
        blur_kernel,
        jax.ShapeDtypeStruct(rows_shape, BF16),
        [wide, scratch],
        flops,
        *field,
        *forward,
    )
    side = 2 * REACH
    part, send_near, send_far = call(
        back_kernel,
        (shape(ext, ext),) + (codes(ext + 1, side),) * 2,
        [scratch],
        flops,
        where,
        blurred,
        got,
        *back,
        scalars=1,
    )
    side_shape = (shape(ext, side),) + (codes(side + 1, side),) * 2
    from_far, from_near = swap_far(send_far, "brick"), swap_near(send_near, "brick")
    total_near, nn, nf = call(partial(gather_side_kernel, 0), side_shape, [], 0, part, from_near)
    total_far, fn, ff = call(partial(gather_side_kernel, 1), side_shape, [], 0, part, from_far, total_near)
    side = REACH
    kept, part, send_near, send_far = call(
        full_kernel,
        (shape(ext, planes), shape(ext, ext), codes(ext + 1, side), codes(ext + 1, side)),
        [wide, scratch, pltpu.VMEM(rows_shape, BF16)],
        2 * flops,
        where,
        *field,
        total_near,
        total_far,
        swap_near(nn, "view"),
        swap_far(nf, "view"),
        swap_near(fn, "view"),
        swap_far(ff, "view"),
        got,
        *forward,
        *back,
        scalars=1,
    )
    total, send_near, send_far = call(
        gather_kernel,
        (shape(ext, planes), codes(side + 1, planes), codes(side + 1, planes)),
        [],
        0,
        part,
        swap_near(send_near, "brick"),
        swap_far(send_far, "brick"),
    )
    lower, upper = call(
        last_kernel,
        (codes(core // 2 + 1, planes),) * 2,
        [pltpu.VMEM((core, planes, size_z), F32)],
        0,
        kept,
        total,
        swap_near(send_near, "view"),
        swap_far(send_far, "view"),
    )
    lower_far, upper_near = swap_far(lower, "view", True), swap_near(upper, "view")
    upper_far, lower_near = swap_far(upper, "view", True), swap_near(lower, "view")
    lower_last, upper_last = swap_near(lower_far, "view"), swap_far(upper_near, "view", True)
    merged = call(
        partial(place_kernel, groups),
        shape(planes, size_y),
        [],
        0,
        lower,
        upper,
        lower_near,
        upper_near,
        lower_far,
        upper_far,
    )
    return pl.pallas_call(
        partial(finish_kernel, groups),
        out_shape=shape(planes, size_y),
        in_specs=[VMEM, VMEM, ANY],
        out_specs=ANY,
        scratch_shapes=[pltpu.VMEM((planes, core, size_z), F32), pltpu.SemaphoreType.DMA((2,))],
        input_output_aliases={2: 0},
        compiler_params=pltpu.CompilerParams(vmem_limit_bytes=36 << 20),
    )(lower_last, upper_last, merged)


def solution(mesh):
    return jax.shard_map(
        per_device,
        mesh=mesh,
        in_specs=(
            P("brick", None, None),
            P("view", "brick", None, None),
            P("view", None, None),
            P("view", None, None),
        ),
        out_specs=P("brick", None, None),
        check_vma=False,
    )
```
